32 devices in a mesh: lat: 8 (over y, x, core), lon: 4 (over z).
Axes of the slice: x: 2, y: 2, z: 4, core: 2. Of those that a mesh axis runs over, the one named last changes fastest.
Arguments:
- height: float32 [2048, 8640], P('lat', 'lon'), may hold values from -6 to 8
- east_vel: float32 [2048, 8640], P('lat', 'lon'), may hold values from -3 to 3
- north_vel: float32 [2048, 8640], P('lat', 'lon'), may hold values from -3 to 3
- sea_depth: float32 [2048, 8640], P('lat', 'lon'), may hold values from 1 to 4
- sea_mask: int32 [2048, 8640], P('lat', 'lon'), may hold values 0 or 1
- forcing: bfloat16 [2, 8, 2048, 8640], P(None, None, 'lat', 'lon'), may hold values from -6 to 6
- thickness: float32 [8], replicated, may hold values from 1 to 10
- cycle_length: int32 [2048], P('lat'), may hold values from 180 to 720
- slot_order: int32 [720], replicated, may hold values from 0 to 719, each once
- love_index: int32 [720], replicated, may hold values from 0 to 63
- love_table: float32 [64], replicated, may hold values from 0.5 to 1.5
Outputs:
- height_out: float32 [2048, 8640], P('lat', 'lon')
- east_out: float32 [2048, 8640], P('lat', 'lon')
- north_out: float32 [2048, 8640], P('lat', 'lon')
- load_coeffs: float32 [2, 720, 720], P(None, 'lon', 'lat')
- sal_field: float32 [2048, 8640], P('lat', 'lon')
The draws below stay inside these ranges and needn't reach their ends.
Inputs may be any that keep to these rules, and one draw needn't show every extreme that they name: `slot_order`: every order appears once.
All inputs are finite; a program needn't handle non-finite values. No bound on the sum of `sea_mask` on one device may be relied on, other than what follows from the above.
Results may differ from the reference program's by a relative error of at most 0.014.
Values may be sent and summed in bfloat16 or wider, within the bound.
No kernel may reach another device: no remote copies, remote signals or barrier semaphores. Data moves between devices by JAX's collectives and lax.ppermute only.
A program may use at most 192 MiB of HBM per device.

```python
import math
import jax
import jax.numpy as jnp
from jax import lax

NLON = 8640
LMAX = 720
LEVELS = 8
ITERS = 10
LOVE_ROWS = 64
LAT_DEV = 256
NLAT = 2048
ORD_DEV = 180


def draw_height(key, part):
    row_ids = jnp.arange(NLAT, dtype=jnp.int32)
    col_ids = jnp.arange(NLON, dtype=jnp.int32)
    sector = NLON // (LMAX // ORD_DEV)
    row_pos = row_ids % LAT_DEV
    row_gap = jnp.minimum(row_pos, LAT_DEV - 1 - row_pos).astype(jnp.float32)
    col_pos = col_ids % sector
    col_gap = jnp.minimum(col_pos, sector - 1 - col_pos).astype(jnp.float32)
    row_edge = jnp.clip(1.0 - row_gap / 24.0, 0.0, 1.0)
    col_edge = jnp.clip(1.0 - col_gap / 24.0, 0.0, 1.0)
    edge_weight = jnp.maximum(row_edge[:, None], col_edge[None, :])
    phase_key, noise_key = jax.random.split(jax.random.fold_in(key, 11))
    phases = jax.random.uniform(phase_key, (2,), jnp.float32, 0.0, 2.0 * math.pi)
    col_angle = (3 * col_ids % NLON).astype(jnp.float32) * (2.0 * math.pi / NLON)
    row_angle = row_ids.astype(jnp.float32) * (2.0 * math.pi / NLAT)
    smooth_part = 1.0 + 0.5 * jnp.cos(col_angle + phases[0])[None, :] * jnp.cos(row_angle + phases[1])[:, None]
    noise_part = jax.random.normal(noise_key, (NLAT, NLON), jnp.float32)
    height_draw = noise_part + 1.5 * edge_weight * smooth_part
    return jnp.clip(height_draw, -6.0, 8.0)


def with_ends(drawn, rng, low, high):
    spot = [jax.random.randint(jax.random.fold_in(rng, axis), (), 0, length) for axis, length in enumerate(drawn.shape)]
    widest = drawn.shape.index(max(drawn.shape))
    beside = spot[:widest] + [(spot[widest] + 1) % drawn.shape[widest]] + spot[widest + 1:]
    return drawn.at[tuple(spot)].set(low).at[tuple(beside)].set(high)


def levels(rng, dims, cuts, least, largest):
    def one(dim, shards_of):
        heights = jax.random.uniform(jax.random.fold_in(jax.random.fold_in(rng, 6), dim), (shards_of,), jnp.float32, least / len(cuts), largest / len(cuts))
        return jnp.repeat(jnp.exp(heights), dims[dim] // shards_of).reshape((-1,) + (1,) * (len(dims) - dim - 1))

    gain = one(*cuts[0])
    for cut in cuts[1:]:
        gain = gain * one(*cut)
    return gain


def gaussian(key, shape, width, limit, pieces=(), held_as=jnp.bfloat16):
    gain = levels(key, shape, pieces, -0.22, 0.18) if pieces else 1.0
    values = jax.random.normal(key, shape, jnp.float32) * width * gain
    return jnp.minimum(jnp.maximum(values, -limit), limit).astype(held_as)


def setup_inputs(seed: int = 0) -> dict:
    streams_of = jax.random.split(jax.random.key(seed), 12)
    height = draw_height(jax.random.fold_in(streams_of[11], 71), 0)
    east_vel = gaussian(streams_of[1], (NLAT, NLON), 0.5, 3.0, ((0, 8), (1, 4)), jnp.float32)
    north_vel = gaussian(streams_of[2], (NLAT, NLON), 0.5, 3.0, ((0, 8), (1, 4)), jnp.float32)
    sea_depth = jnp.clip(jnp.exp(math.log(4.0) - 1.3862944 * jax.random.uniform(streams_of[3], (NLAT, NLON), jnp.float32) ** levels(streams_of[3], (NLAT, NLON), ((0, 8), (1, 4)), -0.2, 0.2)), 1.0, 4.0)
    sea_mask = with_ends((jax.random.randint(streams_of[4], (NLAT, NLON), 0, 16) < 15).astype(jnp.int32), jax.random.fold_in(streams_of[4], 1), 0, 1)
    forcing = gaussian(streams_of[5], (2, LEVELS, NLAT, NLON), 1.0, 6.0, ((2, 8), (3, 4)))
    thickness = jnp.clip(jnp.exp(jax.random.uniform(streams_of[6], (LEVELS,), jnp.float32, math.log(1.0), math.log(10.0))), 1.0, 10.0)
    cycle_length = with_ends(jax.random.randint(streams_of[7], (NLAT,), LMAX // 4, LMAX + 1), jax.random.fold_in(streams_of[7], 1), LMAX // 4, LMAX).astype(jnp.int32)
    slot_order = jax.random.permutation(streams_of[8], LMAX).astype(jnp.int32)
    love_index = with_ends(jax.random.randint(streams_of[9], (LMAX,), 0, LOVE_ROWS), jax.random.fold_in(streams_of[9], 1), 0, LOVE_ROWS - 1).astype(jnp.int32)
    love_table = jnp.clip(jax.random.uniform(streams_of[10], (LOVE_ROWS,), jnp.float32, 0.5, 1.5), 0.5, 1.5)
    return {"height": height, "east_vel": east_vel, "north_vel": north_vel, "sea_depth": sea_depth, "sea_mask": sea_mask, "forcing": forcing, "thickness": thickness, "cycle_length": cycle_length, "slot_order": slot_order, "love_index": love_index, "love_table": love_table}


time_step = 0.6
drag_coeff = 0.5
tide_speed = 0.1
coriolis_scale = 0.8
degree_block = 24
rescale_limit = 1e+20
rescale_log = 20.0 * math.log(10.0)

def cycle_geometry(row_ids, cycle_count):
    latitude = (row_ids.astype(jnp.float32) + 0.5) * (math.pi / cycle_count) - 0.5 * math.pi
    return (jnp.sin(latitude), jnp.cos(latitude))

def start_logs():
    counter = jnp.arange(LMAX).astype(jnp.float32)
    log_terms = jnp.where(counter > 0.0, 0.5 * jnp.log((2.0 * counter + 1.0) / jnp.maximum(2.0 * counter, 1.0)), 0.0)
    return jnp.cumsum(log_terms)

def next_row(degree, order_col, sine_row, prev_one, prev_two, scale_log):
    deg_gap = degree * degree - order_col * order_col
    past_one = degree >= order_col + 1.0
    past_two = degree >= order_col + 2.0
    lead_sq = jnp.where(past_one, (4.0 * degree * degree - 1.0) / jnp.where(past_one, deg_gap, 1.0), 0.0)
    lag_num = (2.0 * degree + 1.0) * ((degree - 1.0) * (degree - 1.0) - order_col * order_col)
    lag_sq = jnp.where(past_two, lag_num / jnp.where(past_two, (2.0 * degree - 3.0) * deg_gap, 1.0), 0.0)
    value_row = jnp.where(degree == order_col, 1.0, jnp.sqrt(lead_sq) * sine_row * prev_one - jnp.sqrt(lag_sq) * prev_two)
    large = jnp.abs(value_row) > rescale_limit
    factor = jnp.where(large, 1.0 / rescale_limit, 1.0)
    value_row = value_row * factor
    carried = prev_one * factor
    scale_log = scale_log + jnp.where(large, rescale_log, 0.0)
    output = value_row * jnp.exp(scale_log)
    return (value_row, carried, scale_log, output)

def wave_table(orders, part_ids, lon_ids):
    phases = (orders[:, None] * lon_ids[None, :] % NLON).astype(jnp.float32) * (2.0 * math.pi / NLON)
    return jnp.where(part_ids[:, None] == 0, jnp.cos(phases), -jnp.sin(phases))

def forward_entries(orders, part_ids, lon_ids):
    return (wave_table(orders, part_ids, lon_ids) / NLON).astype(jnp.bfloat16)

def inverse_entries(orders, part_ids, lon_ids):
    weight_gain = jnp.where(orders == 0, 1.0, 2.0)
    return (weight_gain[:, None] * wave_table(orders, part_ids, lon_ids)).astype(jnp.bfloat16)

def legendre_scan(orders_f, log_m, sines, cosines):
    order_col = orders_f[:, None]
    start_scale = log_m[:, None] + order_col * jnp.log(cosines)[None, :]
    sine_row = sines[None, :]

    def advance(carry, degree_id):
        prev_one, prev_two, scale_log = carry
        value_row, carried, scale_log, output = next_row(degree_id.astype(jnp.float32), order_col, sine_row, prev_one, prev_two, scale_log)
        return ((value_row, carried, scale_log), output.astype(jnp.bfloat16))
    empty = jnp.zeros(start_scale.shape, jnp.float32)
    finished, tables = lax.scan(advance, (empty, empty, start_scale), jnp.arange(LMAX, dtype=jnp.int32))
    return jnp.transpose(tables, (1, 0, 2))

def reference(height, east_vel, north_vel, sea_depth, sea_mask, forcing, thickness, cycle_length, slot_order, love_index, love_table):
    row_ids = jnp.arange(NLAT, dtype=jnp.int32)
    sines, cosines = cycle_geometry(row_ids, NLAT)
    inside = (row_ids > 0) & (row_ids < NLAT - 1)
    wet_cells = jnp.where(inside[:, None] & (sea_mask > 0), 1.0, 0.0).astype(jnp.float32)
    level_weights = thickness / jnp.sum(thickness)
    east_push = jnp.zeros(height.shape, jnp.float32)
    north_push = jnp.zeros(height.shape, jnp.float32)
    for level in range(LEVELS):
        east_push = east_push + level_weights[level] * forcing[0, level].astype(jnp.float32)
        north_push = north_push + level_weights[level] * forcing[1, level].astype(jnp.float32)
    coriolis = coriolis_scale * sines[:, None]
    east, north = (east_vel, north_vel)
    for substep in range(ITERS):
        east_flux = sea_depth * east
        north_flux = sea_depth * north
        padded = jnp.pad(north_flux, ((1, 1), (0, 0)))
        height = height - time_step * wet_cells * (0.5 * (jnp.roll(east_flux, -1, 1) - jnp.roll(east_flux, 1, 1) + (padded[2:] - padded[:-2])))
        padded = jnp.pad(height, ((1, 1), (0, 0)))
        east_slope = 0.5 * (jnp.roll(height, -1, 1) - jnp.roll(height, 1, 1))
        north_slope = 0.5 * (padded[2:] - padded[:-2])
        flow_speed = jnp.sqrt(east * east + north * north + tide_speed * tide_speed)
        damping = 1.0 + time_step * drag_coeff * flow_speed / sea_depth
        east_new = wet_cells * (east + time_step * (coriolis * north - east_slope + east_push)) / damping
        north = wet_cells * (north + time_step * (-coriolis * east - north_slope + north_push)) / damping
        east = east_new
    surface_load = (wet_cells * height).astype(jnp.bfloat16)
    column_ids = jnp.arange(2 * LMAX, dtype=jnp.int32)
    orders = column_ids % LMAX
    part_ids = column_ids // LMAX
    lon_ids = jnp.arange(NLON, dtype=jnp.int32)
    spectra = jnp.dot(forward_entries(orders, part_ids, lon_ids), surface_load.T, preferred_element_type=jnp.float32).reshape(2, LMAX, NLAT)
    retained = jnp.arange(LMAX, dtype=jnp.int32)[:, None] < cycle_length[None, :]
    weight_lat = 0.5 * cosines * (math.pi / NLAT)
    weighted = jnp.where(retained[None], spectra * weight_lat[None, None, :], 0.0).astype(jnp.bfloat16)
    log_starts = start_logs()
    load_factor = love_table[love_index]

    def order_block(block_id):
        block_orders = block_id * degree_block + jnp.arange(degree_block, dtype=jnp.int32)
        tables = legendre_scan(block_orders.astype(jnp.float32), log_starts[block_orders], sines, cosines).astype(jnp.float32)
        block_weighted = lax.dynamic_slice(weighted, (jnp.int32(0), (block_id * degree_block).astype(jnp.int32), jnp.int32(0)), (2, degree_block, NLAT))
        sums = jnp.einsum('knj,pkj->pkn', tables, block_weighted.astype(jnp.float32), precision=lax.Precision.HIGHEST)
        coefficients = sums * load_factor[None, None, :]
        scaled = coefficients.astype(jnp.bfloat16).astype(jnp.float32)
        synthesis = jnp.einsum('knj,pkn->pkj', tables, scaled, precision=lax.Precision.HIGHEST).astype(jnp.bfloat16)
        return (synthesis, coefficients)
    synthesis, coefficients = lax.map(order_block, jnp.arange(LMAX // degree_block, dtype=jnp.int32))
    synthesis = jnp.transpose(synthesis, (1, 0, 2, 3)).reshape(2 * LMAX, NLAT)
    coefficients = jnp.transpose(coefficients, (1, 0, 2, 3)).reshape(2, LMAX, LMAX)
    load_coeffs = math.sqrt(NLON * NLAT) * coefficients[:, slot_order, :]
    sal_field = jnp.dot(synthesis.T, inverse_entries(orders, part_ids, lon_ids), preferred_element_type=jnp.float32)
    return (height, east, north, load_coeffs, sal_field)
```

```python
import functools
import math

import jax
import jax.numpy as jnp
import numpy as np
from jax import lax
from jax.experimental import pallas as pl
from jax.experimental.pallas import tpu as pltpu
from jax.sharding import PartitionSpec as P

NLON = 8640
LMAX = 720
LEVELS = 8
ITERS = 10
LOVE_ROWS = 64

time_step = 0.6
drag_coeff = 0.5
tide_speed = 0.1
coriolis_scale = 0.8

MARGIN = 2 * ITERS
STRIP = 24
TOP = 32
BT = 3
FIELDS = 7
GROUP = 8
CHUNK = 32
NCHUNK = -(-LMAX // CHUNK)
CROWS = CHUNK * GROUP
LIMIT = 1e10
SHRINK = 1e-20
SHRINK_LOG = 20.0 * math.log(10.0)
VMEM_LIMIT = 60 * 1024 * 1024


def tile_count(cols):
    tiles = -(-(cols + 2 * STRIP) // 128)
    while cols % tiles or cols // tiles % 8:
        tiles += 1
    return tiles


def wet_of(in_ref, mask):
    return jnp.where((in_ref[...] > 0.0) & (mask > 0), 1.0, 0.0)


def push_of(weight_ref, f_ref, part):
    total = weight_ref[0] * f_ref[part, 0].astype(jnp.float32)
    for level in range(1, LEVELS):
        total += weight_ref[level] * f_ref[part, level].astype(jnp.float32)
    return time_step * total


def edge_kernel(weight_ref, h_ref, e_ref, n_ref, d_ref, m_ref, f_ref, in_ref, out_ref):
    out_ref[0, 0] = 0.3 * h_ref[...]
    out_ref[0, 1] = e_ref[...]
    out_ref[0, 2] = n_ref[...]
    out_ref[0, 3] = d_ref[...]
    out_ref[0, 4] = wet_of(in_ref, m_ref[...])
    out_ref[0, 5] = push_of(weight_ref, f_ref, 0)
    out_ref[0, 6] = push_of(weight_ref, f_ref, 1)


def edges(weights, fields, forcing, inside):
    cols, rows = fields[0].shape
    at = lambda g: g * (cols // STRIP - 1)
    return pl.pallas_call(
        edge_kernel,
        grid=(2,),
        in_specs=[pl.BlockSpec(memory_space=pltpu.SMEM)]
        + [pl.BlockSpec((STRIP, rows), lambda g: (at(g), 0))] * 5
        + [pl.BlockSpec((2, LEVELS, STRIP, rows), lambda g: (0, 0, at(g), 0))]
        + [pl.BlockSpec(inside.shape, lambda g: (0, 0))],
        out_specs=pl.BlockSpec((1, FIELDS, STRIP, rows), lambda g: (g, 0, 0, 0)),
        out_shape=jax.ShapeDtypeStruct((2, FIELDS, STRIP, rows), jnp.float32),
        name="edges",
    )(weights, *fields, forcing, inside)


def push_kernel(weight_ref, f_ref, out_ref):
    out_ref[0] = push_of(weight_ref, f_ref, 0)
    out_ref[1] = push_of(weight_ref, f_ref, 1)


def push(weights, forcing):
    _, _, cols, rows = forcing.shape
    width = 9 * STRIP
    return pl.pallas_call(
        push_kernel,
        grid=(-(-cols // width),),
        in_specs=[
            pl.BlockSpec(memory_space=pltpu.SMEM),
            pl.BlockSpec((2, LEVELS, width, rows), lambda g: (0, 0, g, 0)),
        ],
        out_specs=pl.BlockSpec((2, width, rows), lambda g: (0, g, 0)),
        out_shape=jax.ShapeDtypeStruct((2, cols, rows), jnp.float32),
        compiler_params=pltpu.CompilerParams(vmem_limit_bytes=VMEM_LIMIT),
        cost_estimate=pl.CostEstimate(
            flops=32 * cols * rows, bytes_accessed=40 * cols * rows, transcendentals=0
        ),
        name="push",
    )(weights, forcing)


def arrange_kernel(tiles, h_ref, e_ref, n_ref, d_ref, m_ref, p_ref, halo_ref, in_ref, out_ref):
    lanes = h_ref.shape[0] // tiles
    for t in range(tiles):
        rows = pl.ds(t, lanes, tiles)
        fields = (
            0.3 * h_ref[rows, :], e_ref[rows, :], n_ref[rows, :], d_ref[rows, :],
            wet_of(in_ref, m_ref[rows, :]), p_ref[0, rows, :], p_ref[1, rows, :],
        )
        for v, field in enumerate(fields):
            rest = halo_ref[v, pl.ds(t, 128 - lanes, tiles), :]
            out_ref[v, t] = jnp.concatenate([field, rest], axis=0).T


def arrange(fields, pushes, halo, inside, tiles):
    cols, rows = fields[0].shape
    return pl.pallas_call(
        functools.partial(arrange_kernel, tiles),
        grid=(rows // 128,),
        in_specs=[pl.BlockSpec((cols, 128), lambda g: (0, g))] * 5
        + [pl.BlockSpec((2, cols, 128), lambda g: (0, 0, g))]
        + [pl.BlockSpec(halo.shape[:2] + (128,), lambda g: (0, 0, g))]
        + [pl.BlockSpec((1, 128), lambda g: (0, g))],
        out_specs=pl.BlockSpec((FIELDS, tiles, 128, 128), lambda g: (0, 0, g, 0)),
        out_shape=jax.ShapeDtypeStruct((FIELDS, tiles, rows, 128), jnp.float32),
        compiler_params=pltpu.CompilerParams(vmem_limit_bytes=VMEM_LIMIT),
        name="arrange",
    )(*fields, pushes, halo, inside)


def ocean_kernel(
    nt, field_ref, spin_ref, low_ref, high_ref, ho_ref, eo_ref, no_ref, lo_ref,
    H, E, N, PE, PN, K, D, A, FE, FN,
):
    step = pl.program_id(0)
    block = field_ref.shape[1]
    rows = field_ref.shape[2]
    lanes = ho_ref.shape[0] // nt
    own = slice(TOP, TOP + rows)

    def put(t, where, height, east, north, depth, wet, push_e, push_n):
        is_wet = wet > 0.0
        H[t + 1, where, :] = height
        E[t, where, :] = east
        N[t, where, :] = north
        PE[t, where, :] = push_e
        PN[t, where, :] = push_n
        K[t, where, :] = jnp.where(is_wet, 0.3 / jnp.where(is_wet, depth, 1.0), jnp.inf)
        D[t, where, :] = depth
        A[t, where, :] = jnp.where(is_wet, 0.09, 0.0)
        FE[t + 1, where, :] = depth * east
        FN[t, where, :] = depth * north

    @pl.when(step < nt // block)
    def ingest():
        for b in range(block):
            t = step * block + b
            put(t, own, *[field_ref[v, b] for v in range(FIELDS)])
            put(t, slice(TOP - STRIP, TOP), *[low_ref[v, b] for v in range(FIELDS)])
            put(t, slice(TOP + rows, TOP + rows + STRIP), *[high_ref[v, b] for v in range(FIELDS)])

    @pl.when(step == nt // block - 1)
    def run():
        def close(ref, tiles):
            for r in tiles:
                here = slice(r * 8, r * 8 + 8)
                ref[0, here, :] = pltpu.roll(ref[nt, here, :], 1, 1)
                ref[nt + 1, here, :] = pltpu.roll(ref[1, here, :], 127, 1)

        def substeps(first_tile, last_tile, count):
            tiles = range(first_tile, last_tile)

            def raise_height(t, carry):
                for r in tiles:
                    here = slice(r * 8, r * 8 + 8)
                    slope = FE[t + 2, here, :] - FE[t, here, :]
                    slope = slope + (FN[t, r * 8 + 1 : r * 8 + 9, :] - FN[t, r * 8 - 1 : r * 8 + 7, :])
                    H[t + 1, here, :] = H[t + 1, here, :] - A[t, here, :] * slope
                return carry

            def turn(t, carry):
                for r in tiles:
                    here = slice(r * 8, r * 8 + 8)
                    spin = spin_ref[here, :]
                    slope = H[t + 2, here, :] - H[t, here, :]
                    rise = H[t + 1, r * 8 + 1 : r * 8 + 9, :] - H[t + 1, r * 8 - 1 : r * 8 + 7, :]
                    east, north = E[t, here, :], N[t, here, :]
                    square = east * east + north * north + tide_speed * tide_speed
                    speed = square * lax.rsqrt(square)
                    damp = pl.reciprocal(1.0 + K[t, here, :] * speed, approx=True)
                    east_new = (east + spin * north - slope + PE[t, here, :]) * damp
                    north_new = (north - spin * east - rise + PN[t, here, :]) * damp
                    E[t, here, :] = east_new
                    N[t, here, :] = north_new
                    depth = D[t, here, :]
                    FE[t + 1, here, :] = depth * east_new
                    FN[t, here, :] = depth * north_new
                return carry

            def one(substep, carry):
                close(FE, tiles)
                lax.fori_loop(0, nt, raise_height, 0)
                close(H, tiles)
                lax.fori_loop(0, nt, turn, 0)
                return carry

            lax.fori_loop(0, count, one, 0)

        substep = 0
        while substep < ITERS:
            reach = lambda k: -(-(MARGIN - 2 * k - 1) // 8)
            count = 1
            while substep + count < ITERS and reach(substep + count) == reach(substep):
                count += 1
            substeps(TOP // 8 - reach(substep), (TOP + rows) // 8 + reach(substep), count)
            substep += count

    @pl.when(step >= nt // block - 1)
    def emit():
        first_row = pl.multiple_of(TOP + (step - (nt // block - 1)) * 128, 8)
        here = pl.ds(first_row, 128)
        for t in range(nt):
            where = pl.ds(t, lanes, nt)
            height = H[t + 1, here, :] * (1.0 / 0.3)
            ho_ref[where, :] = height.T[:lanes]
            eo_ref[where, :] = E[t, here, :].T[:lanes]
            no_ref[where, :] = N[t, here, :].T[:lanes]
            lo_ref[:, t * 128 : (t + 1) * 128] = jnp.where(A[t, here, :] > 0.0, height, 0.0).astype(
                jnp.bfloat16
            )


def ocean(cols, fields, spin, low, high):
    _, nt, rows, _ = fields.shape
    block = BT if nt % BT == 0 else 1
    whole = lambda shape: pl.BlockSpec(
        shape, lambda g: (0,) * len(shape), pipeline_mode=pl.Buffered(1)
    )
    steps = nt // block
    by_tile = lambda n: pl.BlockSpec(
        (FIELDS, block, n, 128), lambda g: (0, jnp.minimum(g, steps - 1), 0, 0)
    )
    band = lambda g: jnp.clip(g - (steps - 1), 0, rows // 128 - 1)
    out_block = pl.BlockSpec((cols, 128), lambda g: (0, band(g)))
    load_block = pl.BlockSpec((128, nt * 128), lambda g: (band(g), 0))
    outs = [jax.ShapeDtypeStruct((cols, rows), jnp.float32)] * 3
    outs.append(jax.ShapeDtypeStruct((rows, nt * 128), jnp.bfloat16))
    plain = pltpu.VMEM((nt, TOP + rows + 32, 128), jnp.float32)
    ringed = pltpu.VMEM((nt + 2, TOP + rows + 32, 128), jnp.float32)
    return pl.pallas_call(
        functools.partial(ocean_kernel, nt),
        grid=(steps + rows // 128 - 1,),
        in_specs=[by_tile(rows), whole(spin.shape), by_tile(STRIP), by_tile(STRIP)],
        out_specs=[out_block] * 3 + [load_block],
        out_shape=outs,
        scratch_shapes=[ringed] + [plain] * 7 + [ringed, plain],
        compiler_params=pltpu.CompilerParams(vmem_limit_bytes=VMEM_LIMIT),
        name="ocean",
    )(fields, spin, low, high)


def legendre_kernel(
    start_ref, w_ref, z_ref, s_ref, co_ref, l_ref, y_ref, c_ref, table, one, two, zed, spread
):
    first_block = start_ref[pl.program_id(0)]
    lats = w_ref.shape[2]
    half = lats // 128
    y_ref[...] = jnp.zeros(y_ref.shape, jnp.float32)
    c_ref[...] = jnp.zeros(c_ref.shape, jnp.float32)
    one[...] = jnp.ones(one.shape, jnp.float32)
    two[...] = jnp.ones(two.shape, jnp.float32)
    zed[...] = z_ref[0]
    row_ids = lax.broadcasted_iota(jnp.int32, (4 * GROUP, CROWS), 0)
    lane_ids = lax.broadcasted_iota(jnp.int32, (4 * GROUP, CROWS), 1)
    order_of = lane_ids % GROUP
    match = (row_ids % GROUP == order_of) & (
        row_ids // (2 * GROUP) == (lane_ids // GROUP + order_of) % 2
    )
    chosen = jnp.where(match, 1.0, 0.0)

    def chunk(c, carry):
        pairs = co_ref[0, c]
        for q in range(2 * CHUNK):
            spread[q] = jnp.broadcast_to(pairs[:, q : q + 1], (GROUP, 128))
        for part in range(CHUNK // 16):
            for t in range(half):
                lanes = slice(t * 128, (t + 1) * 128)
                now, old, scale_log = one[:, lanes], two[:, lanes], zed[:, lanes]
                sines = s_ref[:, lanes]
                large = jnp.maximum(jnp.abs(now), jnp.abs(old)) > LIMIT
                factor = jnp.where(large, SHRINK, 1.0)
                now, old = now * factor, old * factor
                scale_log = scale_log + jnp.where(large, SHRINK_LOG, 0.0)
                scale = jnp.exp(scale_log)
                rows = []
                for q in range(part * 16, part * 16 + 16):
                    value = (spread[q] * sines) * now - spread[CHUNK + q] * old
                    old, now = now, value
                    rows.append(value * scale)
                for q in range(0, 16, 2):
                    at = (part * 16 + q) * GROUP
                    table[at : at + 2 * GROUP, lanes] = jnp.concatenate(
                        [rows[q], rows[q + 1]], axis=0
                    ).astype(jnp.bfloat16)
                one[:, lanes], two[:, lanes], zed[:, lanes] = now, old, scale_log
        values = table[...]
        sums = lax.dot_general(
            w_ref[0], values, (((1,), (1,)), ((), ())), preferred_element_type=jnp.float32
        )
        degree_gap = (c * CHUNK - first_block * GROUP) + (lane_ids // GROUP - order_of)
        gain = jnp.where(degree_gap >= 0, chosen, 0.0) * l_ref[c]
        sums = jnp.where(gain != 0.0, sums * gain, 0.0)
        by_part = sums[: 2 * GROUP] + sums[2 * GROUP :]
        for p in range(2):
            c_ref[0, c, p : p + 1, :] = jnp.sum(
                by_part[p * GROUP : (p + 1) * GROUP], axis=0, keepdims=True
            )
        y_ref[0] += jnp.dot(
            sums.astype(jnp.bfloat16), values, preferred_element_type=jnp.float32
        )
        return carry

    first_chunk = jnp.minimum(first_block * GROUP // CHUNK, NCHUNK)
    lax.fori_loop(first_chunk, NCHUNK, chunk, 0)


def legendre(starts, weights, logs, sines, coeffs, loads):
    groups, _, lats = weights.shape
    by_group = lambda x: pl.BlockSpec(
        (1,) + x.shape[1:], lambda g: (g,) + (0,) * (x.ndim - 1)
    )
    whole = lambda x: pl.BlockSpec(x.shape, lambda g: (0,) * x.ndim)
    outs = [
        jax.ShapeDtypeStruct((groups, 4 * GROUP, lats), jnp.float32),
        jax.ShapeDtypeStruct((groups, NCHUNK, 2, CROWS), jnp.float32),
    ]
    return pl.pallas_call(
        legendre_kernel,
        grid=(groups,),
        in_specs=[
            pl.BlockSpec(memory_space=pltpu.SMEM),
            by_group(weights),
            by_group(logs),
            whole(sines),
            by_group(coeffs),
            whole(loads),
        ],
        out_specs=[by_group(x) for x in outs],
        out_shape=outs,
        scratch_shapes=[
            pltpu.VMEM((CROWS, lats), jnp.bfloat16),
            pltpu.VMEM((GROUP, lats), jnp.float32),
            pltpu.VMEM((GROUP, lats), jnp.float32),
            pltpu.VMEM((GROUP, lats), jnp.float32),
            pltpu.VMEM((2 * CHUNK, GROUP, 128), jnp.float32),
        ],
        compiler_params=pltpu.CompilerParams(vmem_limit_bytes=VMEM_LIMIT),
        name="legendre",
    )(starts, weights, logs, sines, coeffs, loads)


def block_of(device, group, devices):
    turned = jnp.where(group % 2 == 0, device, devices - 1 - device)
    return group * devices + turned


def order_layout(devices):
    groups = -(-(LMAX // GROUP) // devices)
    device, group, part, within = np.meshgrid(
        np.arange(devices), np.arange(groups), np.arange(2), np.arange(GROUP), indexing="ij"
    )
    block = group * devices + np.where(group % 2 == 0, device, devices - 1 - device)
    return groups, (block * GROUP + within).reshape(-1), part.reshape(-1)


def sector_table(orders, parts, cols):
    phases = (orders[:, None] * np.arange(cols)[None, :] % NLON) * (2.0 * np.pi / NLON)
    table = np.where(parts[:, None] == 0, np.cos(phases), -np.sin(phases))
    return np.where(orders[:, None] < LMAX, table, 0.0).astype(jnp.bfloat16)


def ring_table(table, tiles):
    ring = np.pad(table, ((0, 0), (0, tiles * 128 - table.shape[1])))
    return ring.reshape(-1, 128, tiles).transpose(0, 2, 1).reshape(ring.shape)


def start_logs():
    t = np.arange(LMAX, dtype=np.float64)
    terms = np.where(t > 0, 0.5 * np.log((2 * t + 1) / np.maximum(2 * t, 1)), 0.0)
    return np.cumsum(terms)


def recurrence(orders):
    degree = jnp.arange(NCHUNK * CHUNK, dtype=jnp.float32).reshape(1, NCHUNK, 1, CHUNK)
    order = orders.astype(jnp.float32)[:, None, :, None]
    gap = degree * degree - order * order
    one, two = degree >= order + 1.0, degree >= order + 2.0
    lead = jnp.where(one, (4.0 * degree * degree - 1.0) / jnp.where(one, gap, 1.0), 0.0)
    lag_num = (2.0 * degree + 1.0) * ((degree - 1.0) * (degree - 1.0) - order * order)
    lag = jnp.where(two, lag_num / jnp.where(two, (2.0 * degree - 3.0) * gap, 1.0), 0.0)
    lead = jnp.sqrt(lead)
    lag = jnp.where(one, jnp.sqrt(lag), -1.0)
    both = jnp.concatenate([lead, lag], axis=3)
    return jnp.pad(both, ((0, 0), (0, 0), (0, 0), (0, 128 - 2 * CHUNK)))


def cycle_geometry(row_ids, cycle_count):
    latitude = (row_ids.astype(jnp.float32) + 0.5) * (math.pi / cycle_count) - 0.5 * math.pi
    return (jnp.sin(latitude), jnp.cos(latitude))


def ring(axis, periodic):
    count = lax.axis_size(axis)
    forward = [(i, i + 1) for i in range(count - 1)]
    if periodic:
        forward.append((count - 1, 0))
    return forward, [(b, a) for a, b in forward]


def local(
    height,
    east_vel,
    north_vel,
    sea_depth,
    sea_mask,
    forcing,
    thickness,
    cycle_length,
    slot_order,
    love_index,
    love_table,
):
    rows, cols = height.shape
    lat_parts, lon_parts = lax.axis_size("lat"), lax.axis_size("lon")
    devices = lat_parts * lon_parts
    cycles = rows * lat_parts
    lat, lon = lax.axis_index("lat"), lax.axis_index("lon")
    bf16, f32 = jnp.bfloat16, jnp.float32

    weights = thickness / jnp.sum(thickness)
    row_ids = lat * rows + jnp.arange(rows, dtype=jnp.int32)
    inside = (row_ids > 0) & (row_ids < cycles - 1)

    tiles = tile_count(cols)
    natural = [x.T for x in (height, east_vel, north_vel, sea_depth, sea_mask)]
    forcing = forcing.transpose(0, 1, 3, 2)
    inside = jnp.where(inside, 1.0, 0.0)[None, :].astype(f32)
    eastward, westward = ring("lon", True)
    northward, southward = ring("lat", False)
    first, last = edges(weights, natural, forcing, inside).astype(bf16)
    left = lax.ppermute(last, "lon", eastward)
    right = lax.ppermute(first, "lon", westward)
    pushes = push(weights, forcing)
    spare = jnp.zeros((FIELDS, tiles * 128 - cols - 2 * STRIP, rows), bf16)
    halo = jnp.concatenate([right, spare, left], axis=1).astype(f32)
    fields = arrange(natural, pushes, halo, inside, tiles)
    low = lax.ppermute(fields[:, :, rows - STRIP :].astype(bf16), "lat", northward).astype(f32)
    high = lax.ppermute(fields[:, :, :STRIP].astype(bf16), "lat", southward).astype(f32)
    wide_rows = lat * rows - TOP + jnp.arange(TOP + rows + 32, dtype=jnp.int32)
    wide_sines, _ = cycle_geometry(wide_rows, cycles)
    spin = (time_step * coriolis_scale) * wide_sines
    spin = jnp.broadcast_to(spin[:, None], (TOP + rows + 32, 128))
    height, east, north, load = ocean(cols, fields, spin, low, high)

    groups, orders, parts = order_layout(devices)
    table = sector_table(orders, parts, cols)
    owned = devices * groups
    orders3 = jnp.asarray(orders.reshape(owned, 2, GROUP)[:, 0], jnp.int32)
    turn = (orders3 * (lon * cols) % NLON).astype(f32) * (2.0 * math.pi / NLON)
    turn_cos, turn_sin = jnp.cos(turn)[:, :, None], jnp.sin(turn)[:, :, None]
    spectra = lax.dot_general(
        jnp.asarray(ring_table(table, tiles)), load, (((1,), (1,)), ((), ())), preferred_element_type=f32
    ).reshape(owned, 2, GROUP, rows)
    spectra = jnp.stack(
        [
            turn_cos * spectra[:, 0] + turn_sin * spectra[:, 1],
            turn_cos * spectra[:, 1] - turn_sin * spectra[:, 0],
        ],
        axis=1,
    )
    _, cosines = cycle_geometry(row_ids, cycles)
    weight_lat = (0.5 / NLON) * cosines * (math.pi / cycles)
    retained = orders3[:, None, :, None] < cycle_length[None, None, None, :]
    weighted = jnp.where(retained, spectra * weight_lat, 0.0).astype(bf16)
    weighted = weighted.reshape(owned * 2 * GROUP, rows)
    mine = lax.psum_scatter(weighted, "lon", scatter_dimension=0, tiled=True)
    mine = lax.all_to_all(mine, "lat", 0, 0, tiled=True)

    mine = mine.reshape(lat_parts, groups * 2 * GROUP, rows)
    flip = jnp.asarray(np.eye(rows)[::-1].astype(bf16))
    hp = lat_parts // 2
    south = mine[:hp].astype(f32)
    north_side = jnp.dot(mine[hp:][::-1], flip, preferred_element_type=f32)
    folded = jnp.stack([south + north_side, south - north_side]).astype(bf16)
    folded = folded.reshape(2, hp, groups, 2 * GROUP, rows).transpose(2, 0, 3, 1, 4)
    folded = folded.reshape(groups, 4 * GROUP, hp * rows)

    device = lon * lat_parts + lat
    starts = jnp.stack([block_of(device, g, devices) for g in range(groups)]).astype(jnp.int32)
    own_orders = starts[:, None] * GROUP + jnp.arange(GROUP, dtype=jnp.int32)[None, :]
    first_logs = jnp.asarray(
        np.pad(start_logs(), (0, owned * GROUP - LMAX)).astype(np.float32)
    )
    own_logs = jnp.stack(
        [lax.dynamic_slice(first_logs, (starts[g] * GROUP,), (GROUP,)) for g in range(groups)]
    )
    half_sines, half_cosines = cycle_geometry(jnp.arange(hp * rows, dtype=jnp.int32), cycles)
    z_start = own_logs[:, :, None] + own_orders.astype(f32)[:, :, None] * jnp.log(half_cosines)
    load_factor = jnp.sum(
        jnp.where(
            love_index[:, None] == jnp.arange(LOVE_ROWS, dtype=jnp.int32)[None, :],
            love_table[None, :],
            0.0,
        ),
        axis=1,
    )
    degree_load = jnp.pad(load_factor, (0, NCHUNK * CHUNK - LMAX)).reshape(NCHUNK, 1, CHUNK, 1)
    degree_load = jnp.broadcast_to(degree_load, (NCHUNK, 1, CHUNK, GROUP)).reshape(NCHUNK, 1, CROWS)
    synth, coeffs = legendre(
        starts,
        folded,
        z_start,
        jnp.broadcast_to(half_sines[None, :], (GROUP, hp * rows)),
        recurrence(own_orders),
        degree_load,
    )

    synth = synth.reshape(groups, 2, 2 * GROUP, hp, rows).transpose(1, 3, 0, 2, 4)
    synth = synth.reshape(2, hp, groups * 2 * GROUP, rows)
    south = (synth[0] + synth[1]).astype(bf16)
    north_side = jnp.dot(
        (synth[0] - synth[1]).astype(bf16), flip, preferred_element_type=f32
    ).astype(bf16)[::-1]
    share = LMAX // lat_parts
    coeffs = coeffs.reshape(groups, NCHUNK, 2, CHUNK, GROUP).transpose(0, 2, 4, 1, 3)
    coeffs = coeffs.reshape(groups * 2 * GROUP, NCHUNK * CHUNK)[:, :LMAX]
    coeffs = coeffs.reshape(groups * 2 * GROUP, lat_parts, share).transpose(1, 0, 2).astype(bf16)
    packet = jnp.concatenate([jnp.concatenate([south, north_side]), coeffs], axis=2)
    packet = lax.all_to_all(packet.reshape(lat_parts * groups * 2 * GROUP, rows + share), "lat", 0, 0, tiled=True)
    packet = lax.all_gather(packet, "lon", axis=0, tiled=True)
    synthesis = packet[:, :rows].reshape(owned, 2, GROUP, rows).astype(f32)

    gain = jnp.where(orders3 == 0, 1.0, 2.0)[:, :, None]
    synthesis = jnp.stack(
        [
            gain * (turn_cos * synthesis[:, 0] - turn_sin * synthesis[:, 1]),
            gain * (turn_sin * synthesis[:, 0] + turn_cos * synthesis[:, 1]),
        ],
        axis=1,
    ).astype(bf16).reshape(owned * 2 * GROUP, rows)
    sal_field = lax.dot_general(
        jnp.asarray(table), synthesis, (((0,), (0,)), ((), ())), preferred_element_type=f32
    )

    per_owner = LMAX // lon_parts
    own_slots = lax.dynamic_slice(slot_order, (lon * per_owner,), (per_owner,))
    found = own_slots[:, None] == orders3.reshape(-1)[None, :]
    by_order = packet[:, rows:].reshape(owned, 2, GROUP, share).transpose(1, 0, 2, 3)
    by_order = by_order.reshape(2, owned * GROUP, share)
    load_coeffs = math.sqrt(NLON * cycles) * jnp.einsum(
        "qm,pmk->pqk", found.astype(bf16), by_order, preferred_element_type=f32
    )
    return (height.T, east.T, north.T, load_coeffs, sal_field.T)


def solution(mesh):
    in_specs = (
        P("lat", "lon"),
        P("lat", "lon"),
        P("lat", "lon"),
        P("lat", "lon"),
        P("lat", "lon"),
        P(None, None, "lat", "lon"),
        P(),
        P("lat"),
        P(),
        P(),
        P(),
    )
    out_specs = (
        P("lat", "lon"),
        P("lat", "lon"),
        P("lat", "lon"),
        P(None, "lon", "lat"),
        P("lat", "lon"),
    )
    return jax.shard_map(local, mesh=mesh, in_specs=in_specs, out_specs=out_specs, check_vma=False)
```

```python
import functools
import math

import jax
import jax.numpy as jnp
import numpy as np
from jax import lax
from jax.experimental import pallas as pl
from jax.experimental.pallas import tpu as pltpu
from jax.sharding import PartitionSpec as P

NLON = 8640
LMAX = 720
LEVELS = 8
ITERS = 10
LOVE_ROWS = 64

time_step = 0.6
drag_coeff = 0.5
tide_speed = 0.1
coriolis_scale = 0.8

MARGIN = 2 * ITERS
STRIP = 24
TOP = 32
BT = 3
FIELDS = 7
GROUP = 8
CHUNK = 32
NCHUNK = -(-LMAX // CHUNK)
HELD = NCHUNK + 1
CROWS = CHUNK * GROUP
LIMIT = 1e10
SHRINK = 1e-20
SHRINK_LOG = 20.0 * math.log(10.0)
VMEM_LIMIT = 60 * 1024 * 1024


def tile_count(cols):
    tiles = -(-(cols + 2 * STRIP) // 128)
    while cols % tiles or cols // tiles % 8:
        tiles += 1
    return tiles


def wet_of(in_ref, mask):
    return jnp.where((in_ref[...] > 0.0) & (mask > 0), 1.0, 0.0)


def push_of(thick_ref, f_ref, part, where=slice(None)):
    total = thick_ref[0]
    pushed = total * f_ref[part, 0, where, :].astype(jnp.float32)
    for level in range(1, LEVELS):
        total = total + thick_ref[level]
        pushed += thick_ref[level] * f_ref[part, level, where, :].astype(jnp.float32)
    return pushed * (time_step / jnp.full((1, pushed.shape[1]), total, jnp.float32))


def edge_kernel(thick_ref, h_ref, e_ref, n_ref, d_ref, m_ref, f_ref, in_ref, out_ref):
    fields = (
        0.3 * h_ref[...], e_ref[...], n_ref[...], d_ref[...], wet_of(in_ref, m_ref[...]),
        push_of(thick_ref, f_ref, 0), push_of(thick_ref, f_ref, 1),
    )
    for v, field in enumerate(fields):
        out_ref[0, v] = field.astype(jnp.bfloat16)


def edges(weights, fields, forcing, inside):
    cols, rows = fields[0].shape
    at = lambda g: g * (cols // STRIP - 1)
    return pl.pallas_call(
        edge_kernel,
        grid=(2,),
        in_specs=[pl.BlockSpec(memory_space=pltpu.SMEM)]
        + [pl.BlockSpec((STRIP, rows), lambda g: (at(g), 0))] * 5
        + [pl.BlockSpec((2, LEVELS, STRIP, rows), lambda g: (0, 0, at(g), 0))]
        + [pl.BlockSpec(inside.shape, lambda g: (0, 0))],
        out_specs=pl.BlockSpec((1, FIELDS, STRIP, rows), lambda g: (g, 0, 0, 0)),
        out_shape=jax.ShapeDtypeStruct((2, FIELDS, STRIP, rows), jnp.bfloat16),
        name="edges",
    )(weights, *fields, forcing, inside)


def push_kernel(thick_ref, f_ref, out_ref):
    def part(i, carry):
        where = pl.ds(pl.multiple_of(i * STRIP, 8), STRIP)
        out_ref[0, where, :] = push_of(thick_ref, f_ref, 0, where)
        out_ref[1, where, :] = push_of(thick_ref, f_ref, 1, where)
        return carry

    lax.fori_loop(0, out_ref.shape[1] // STRIP, part, 0)


def push(weights, forcing):
    _, _, cols, rows = forcing.shape
    width = 15 * STRIP
    return pl.pallas_call(
        push_kernel,
        grid=(-(-cols // width),),
        in_specs=[
            pl.BlockSpec(memory_space=pltpu.SMEM),
            pl.BlockSpec((2, LEVELS, width, rows), lambda g: (0, 0, g, 0)),
        ],
        out_specs=pl.BlockSpec((2, width, rows), lambda g: (0, g, 0)),
        out_shape=jax.ShapeDtypeStruct((2, cols, rows), jnp.float32),
        compiler_params=pltpu.CompilerParams(vmem_limit_bytes=VMEM_LIMIT),
        cost_estimate=pl.CostEstimate(
            flops=32 * cols * rows, bytes_accessed=40 * cols * rows, transcendentals=0
        ),
        name="push",
    )(weights, forcing)


def arrange_kernel(
    tiles, h_ref, e_ref, n_ref, d_ref, m_ref, p_ref, east_ref, west_ref, in_ref,
    out_ref, first_ref, last_ref, halo_ref,
):
    lanes = h_ref.shape[0] // tiles

    @pl.when(pl.program_id(0) == 0)
    def start():
        halo_ref[...] = jnp.zeros(halo_ref.shape, jnp.float32)
        for v in range(FIELDS):
            halo_ref[v, :STRIP, :] = east_ref[v].astype(jnp.float32)
            halo_ref[v, halo_ref.shape[1] - STRIP :, :] = west_ref[v].astype(jnp.float32)

    for b in range(out_ref.shape[1]):
        t = pl.program_id(0) * out_ref.shape[1] + b
        rows = pl.ds(t, lanes, tiles)
        fields = (
            0.3 * h_ref[rows, :], e_ref[rows, :], n_ref[rows, :], d_ref[rows, :],
            wet_of(in_ref, m_ref[rows, :]), p_ref[0, rows, :], p_ref[1, rows, :],
        )
        for v, field in enumerate(fields):
            rest = halo_ref[v, pl.ds(t, 128 - lanes, tiles), :]
            turned = jnp.concatenate([field, rest], axis=0).T
            out_ref[v, b] = turned
            first_ref[v, b] = turned[:STRIP].astype(jnp.bfloat16)
            last_ref[v, b] = turned[128 - STRIP :].astype(jnp.bfloat16)


def arrange(fields, pushes, east, west, inside, tiles, at):
    cols, rows = fields[0].shape
    block = BT if tiles % BT == 0 else 1
    edge = jax.ShapeDtypeStruct((FIELDS, tiles, STRIP, 128), jnp.bfloat16)
    out_block = lambda n: pl.BlockSpec((FIELDS, block, n, 128), lambda g: (0, g, 0, 0))
    halo_block = pl.BlockSpec((FIELDS, STRIP, 128), lambda g: (0, 0, at))
    return pl.pallas_call(
        functools.partial(arrange_kernel, tiles),
        grid=(tiles // block,),
        in_specs=[pl.BlockSpec((cols, 128), lambda g: (0, at))] * 5
        + [pl.BlockSpec((2, cols, 128), lambda g: (0, 0, at))]
        + [halo_block] * 2
        + [pl.BlockSpec((1, 128), lambda g: (0, at))],
        out_specs=[out_block(128), out_block(STRIP), out_block(STRIP)],
        out_shape=[jax.ShapeDtypeStruct((FIELDS, tiles, 128, 128), jnp.float32), edge, edge],
        scratch_shapes=[pltpu.VMEM((FIELDS, tiles * 128 - cols, 128), jnp.float32)],
        compiler_params=pltpu.CompilerParams(vmem_limit_bytes=VMEM_LIMIT),
        cost_estimate=pl.CostEstimate(
            flops=64 * cols * 128, bytes_accessed=64 * cols * 128, transcendentals=0
        ),
        name="arrange",
    )(*fields, pushes, east, west, inside)


def ocean_kernel(nt, parts, *refs):
    field_refs, refs = refs[:parts], refs[parts:]
    spin_ref, low_ref, high_ref, ho_ref, eo_ref, no_ref, lo_ref, *refs = refs
    H, E, N, PE, PN, K, D, A, FE, FN = refs
    step = pl.program_id(0)
    block = field_refs[0].shape[1]
    rows = parts * 128
    lanes = ho_ref.shape[0] // nt

    def put(t, where, height, east, north, depth, wet, push_e, push_n):
        is_wet = wet > 0.0
        H[t + 1, where, :] = height
        E[t, where, :] = east
        N[t, where, :] = north
        PE[t, where, :] = push_e
        PN[t, where, :] = push_n
        K[t, where, :] = jnp.where(is_wet, 0.3 / jnp.where(is_wet, depth, 1.0), jnp.inf)
        D[t, where, :] = depth
        A[t, where, :] = jnp.where(is_wet, 0.09, 0.0)
        FE[t + 1, where, :] = depth * east
        FN[t, where, :] = depth * north

    @pl.when(step < nt // block)
    def ingest():
        for b in range(block):
            t = step * block + b
            for part, ref in enumerate(field_refs):
                where = slice(TOP + part * 128, TOP + (part + 1) * 128)
                put(t, where, *[ref[v, b] for v in range(FIELDS)])
            put(t, slice(TOP - STRIP, TOP), *[low_ref[v, b].astype(jnp.float32) for v in range(FIELDS)])
            put(t, slice(TOP + rows, TOP + rows + STRIP), *[high_ref[v, b].astype(jnp.float32) for v in range(FIELDS)])

    @pl.when(step == nt // block - 1)
    def run():
        def close(ref, tiles):
            for r in tiles:
                here = slice(r * 8, r * 8 + 8)
                ref[0, here, :] = pltpu.roll(ref[nt, here, :], 1, 1)
                ref[nt + 1, here, :] = pltpu.roll(ref[1, here, :], 127, 1)

        def substeps(first_tile, last_tile, count):
            tiles = range(first_tile, last_tile)

            def raise_height(t, carry):
                for r in tiles:
                    here = slice(r * 8, r * 8 + 8)
                    slope = FE[t + 2, here, :] - FE[t, here, :]
                    slope = slope + (FN[t, r * 8 + 1 : r * 8 + 9, :] - FN[t, r * 8 - 1 : r * 8 + 7, :])
                    H[t + 1, here, :] = H[t + 1, here, :] - A[t, here, :] * slope
                return carry

            def turn(t, carry):
                for r in tiles:
                    here = slice(r * 8, r * 8 + 8)
                    spin = spin_ref[here, :]
                    slope = H[t + 2, here, :] - H[t, here, :]
                    rise = H[t + 1, r * 8 + 1 : r * 8 + 9, :] - H[t + 1, r * 8 - 1 : r * 8 + 7, :]
                    east, north = E[t, here, :], N[t, here, :]
                    square = east * east + north * north + tide_speed * tide_speed
                    speed = square * lax.rsqrt(square)
                    damp = pl.reciprocal(1.0 + K[t, here, :] * speed, approx=True)
                    east_new = (east + spin * north - slope + PE[t, here, :]) * damp
                    north_new = (north - spin * east - rise + PN[t, here, :]) * damp
                    E[t, here, :] = east_new
                    N[t, here, :] = north_new
                    depth = D[t, here, :]
                    FE[t + 1, here, :] = depth * east_new
                    FN[t, here, :] = depth * north_new
                return carry

            def one(substep, carry):
                close(FE, tiles)
                lax.fori_loop(0, nt, raise_height, 0)
                close(H, tiles)
                lax.fori_loop(0, nt, turn, 0)
                return carry

            lax.fori_loop(0, count, one, 0)

        substep = 0
        while substep < ITERS:
            reach = lambda k: -(-(MARGIN - 2 * k - 1) // 8)
            count = 1
            while substep + count < ITERS and reach(substep + count) == reach(substep):
                count += 1
            substeps(TOP // 8 - reach(substep), (TOP + rows) // 8 + reach(substep), count)
            substep += count

    @pl.when(step >= nt // block - 1)
    def emit():
        first_row = pl.multiple_of(TOP + (step - (nt // block - 1)) * 128, 8)
        here = pl.ds(first_row, 128)
        for t in range(nt):
            where = pl.ds(t, lanes, nt)
            height = H[t + 1, here, :] * (1.0 / 0.3)
            ho_ref[where, :] = height.T[:lanes]
            eo_ref[where, :] = E[t, here, :].T[:lanes]
            no_ref[where, :] = N[t, here, :].T[:lanes]
            lo_ref[:, t * 128 : (t + 1) * 128] = jnp.where(A[t, here, :] > 0.0, height, 0.0).astype(
                jnp.bfloat16
            )


def ocean(cols, fields, spin, low, high):
    nt, rows = fields[0].shape[1], 128 * len(fields)
    block = BT if nt % BT == 0 else 1
    whole = lambda shape: pl.BlockSpec(
        shape, lambda g: (0,) * len(shape), pipeline_mode=pl.Buffered(1)
    )
    steps = nt // block
    by_tile = lambda n: pl.BlockSpec(
        (FIELDS, block, n, 128), lambda g: (0, jnp.minimum(g, steps - 1), 0, 0)
    )
    band = lambda g: jnp.clip(g - (steps - 1), 0, rows // 128 - 1)
    out_block = pl.BlockSpec((cols, 128), lambda g: (0, band(g)))
    load_block = pl.BlockSpec((128, nt * 128), lambda g: (band(g), 0))
    outs = [jax.ShapeDtypeStruct((cols, rows), jnp.float32)] * 3
    outs.append(jax.ShapeDtypeStruct((rows, nt * 128), jnp.bfloat16))
    plain = pltpu.VMEM((nt, TOP + rows + 32, 128), jnp.float32)
    ringed = pltpu.VMEM((nt + 2, TOP + rows + 32, 128), jnp.float32)
    return pl.pallas_call(
        functools.partial(ocean_kernel, nt, len(fields)),
        grid=(steps + rows // 128 - 1,),
        in_specs=[by_tile(128)] * len(fields) + [whole(spin.shape), by_tile(STRIP), by_tile(STRIP)],
        out_specs=[out_block] * 3 + [load_block],
        out_shape=outs,
        scratch_shapes=[ringed] + [plain] * 7 + [ringed, plain],
        compiler_params=pltpu.CompilerParams(vmem_limit_bytes=VMEM_LIMIT),
        name="ocean",
    )(*fields, spin, low, high)


def legendre_kernel(
    start_ref, w_ref, z_ref, s_ref, co_ref, l_ref, y_ref, c_ref,
    table_a, table_b, partial_a, partial_b, one, two, zed, scales, folded, spread,
):
    first_block = start_ref[pl.program_id(0)]
    lats = w_ref.shape[2]
    half = lats // 128
    y_ref[...] = jnp.zeros(y_ref.shape, jnp.float32)
    c_ref[...] = jnp.zeros(c_ref.shape, jnp.float32)
    table_b[...] = jnp.zeros(table_b.shape, jnp.bfloat16)
    partial_b[...] = jnp.zeros(partial_b.shape, jnp.float32)
    one[...] = jnp.ones(one.shape, jnp.float32)
    two[...] = jnp.ones(two.shape, jnp.float32)
    zed[...] = z_ref[0]
    row_ids = lax.broadcasted_iota(jnp.int32, (4 * GROUP, CROWS), 0)
    lane_ids = lax.broadcasted_iota(jnp.int32, (4 * GROUP, CROWS), 1)
    order_of = lane_ids % GROUP
    match = (row_ids % GROUP == order_of) & (
        row_ids // (2 * GROUP) == (lane_ids // GROUP + order_of) % 2
    )
    chosen = jnp.where(match, 1.0, 0.0)
    first_part = (row_ids // GROUP) % 2 == 0
    degree_of = (lane_ids // GROUP - order_of - first_block * GROUP)[:1]
    is_even = lax.broadcasted_iota(jnp.int32, (GROUP, lats), 0) % 2 == 0
    for p in range(2):
        even = w_ref[0, p * GROUP : (p + 1) * GROUP, :]
        odd = w_ref[0, (2 + p) * GROUP : (3 + p) * GROUP, :]
        folded[0, p] = jnp.where(is_even, even, odd)
        folded[1, p] = jnp.where(is_even, odd, even)

    def build(c, table, partial, between):
        pairs = co_ref[0, c]
        for q in range(2 * CHUNK):
            spread[q] = jnp.broadcast_to(pairs[:, q : q + 1], (GROUP, 128))
        tiles = [slice(t * 128, (t + 1) * 128) for t in range(half)]
        for part in range(CHUNK // 16):
            between(part)
            now, old = [one[:, x] for x in tiles], [two[:, x] for x in tiles]
            for t, lanes in enumerate(tiles):
                large = jnp.maximum(jnp.abs(now[t]), jnp.abs(old[t])) > LIMIT
                factor = jnp.where(large, SHRINK, 1.0)
                now[t], old[t] = now[t] * factor, old[t] * factor
                scale_log = zed[:, lanes] + jnp.where(large, SHRINK_LOG, 0.0)
                zed[:, lanes] = scale_log
                scales[:, lanes] = jnp.exp(scale_log)
            before = None
            for q in range(part * 16, part * 16 + 16):
                lead, lag = spread[q], spread[CHUNK + q]
                totals, rows = [None, None], []
                for t, lanes in enumerate(tiles):
                    value = (lead * s_ref[:, lanes]) * now[t] - lag * old[t]
                    old[t], now[t] = now[t], value
                    value = value * scales[:, lanes]
                    rows.append(value)
                    for p in range(2):
                        term = value * folded[q % 2, p, :, lanes]
                        totals[p] = term if t == 0 else totals[p] + term
                for p in range(2):
                    partial[p, q * GROUP : (q + 1) * GROUP, :] = totals[p]
                if q % 2:
                    for t, lanes in enumerate(tiles):
                        table[(q - 1) * GROUP : (q + 1) * GROUP, lanes] = jnp.concatenate(
                            [before[t], rows[t]], axis=0
                        ).astype(jnp.bfloat16)
                before = rows
            for t, lanes in enumerate(tiles):
                one[:, lanes], two[:, lanes] = now[t], old[t]

    def sums_of(c, partial):
        ones = jnp.ones((GROUP, 128), jnp.bfloat16)
        across = lambda x: lax.dot_general(
            ones, x, (((1,), (1,)), ((), ())), preferred_element_type=jnp.float32
        )
        gain = jnp.where(degree_of + c * CHUNK >= 0, l_ref[c], 0.0)
        sums = []
        for p in range(2):
            high = partial[p].astype(jnp.bfloat16)
            low = (partial[p] - high.astype(jnp.float32)).astype(jnp.bfloat16)
            total = (across(high) + across(low))[:1]
            total = jnp.where(gain != 0.0, total * gain, 0.0)
            c_ref[0, c, p : p + 1, :] = total
            sums.append(total)
        return (jnp.where(first_part, sums[0], sums[1]) * chosen).astype(jnp.bfloat16)

    def user(c, table, partial):
        held = []
        count = CHUNK // 16 - 1

        def piece(part):
            if part == 0:
                held.append(sums_of(c, partial))
            else:
                width = lats // count
                lanes = slice((part - 1) * width, part * width)
                y_ref[0, :, lanes] += jnp.dot(
                    held[0], table[:, lanes], preferred_element_type=jnp.float32
                )

        return piece

    first_chunk = first_block * GROUP // CHUNK

    def pair(i, carry):
        c = first_chunk + 2 * i
        build(c, table_a, partial_a, user(jnp.maximum(c - 1, 0), table_b, partial_b))
        build(c + 1, table_b, partial_b, user(c, table_a, partial_a))
        return carry

    count = jnp.maximum(NCHUNK - first_chunk + 1, 0) // 2
    lax.fori_loop(0, count, pair, 0)

    @pl.when(count > 0)
    def last():
        piece = user(first_chunk + 2 * count - 1, table_b, partial_b)
        for part in range(CHUNK // 16):
            piece(part)


def legendre(starts, weights, logs, sines, coeffs, loads):
    groups, _, lats = weights.shape
    by_group = lambda x: pl.BlockSpec(
        (1,) + x.shape[1:], lambda g: (g,) + (0,) * (x.ndim - 1)
    )
    whole = lambda x: pl.BlockSpec(x.shape, lambda g: (0,) * x.ndim)
    outs = [
        jax.ShapeDtypeStruct((groups, 4 * GROUP, lats), jnp.float32),
        jax.ShapeDtypeStruct((groups, HELD, 2, CROWS), jnp.float32),
    ]
    return pl.pallas_call(
        legendre_kernel,
        grid=(groups,),
        in_specs=[
            pl.BlockSpec(memory_space=pltpu.SMEM),
            by_group(weights),
            by_group(logs),
            whole(sines),
            by_group(coeffs),
            whole(loads),
        ],
        out_specs=[by_group(x) for x in outs],
        out_shape=outs,
        scratch_shapes=[
            pltpu.VMEM((CROWS, lats), jnp.bfloat16),
            pltpu.VMEM((CROWS, lats), jnp.bfloat16),
            pltpu.VMEM((2, CROWS, 128), jnp.float32),
            pltpu.VMEM((2, CROWS, 128), jnp.float32),
            pltpu.VMEM((GROUP, lats), jnp.float32),
            pltpu.VMEM((GROUP, lats), jnp.float32),
            pltpu.VMEM((GROUP, lats), jnp.float32),
            pltpu.VMEM((GROUP, lats), jnp.float32),
            pltpu.VMEM((2, 2, GROUP, lats), jnp.float32),
            pltpu.VMEM((2 * CHUNK, GROUP, 128), jnp.float32),
        ],
        compiler_params=pltpu.CompilerParams(vmem_limit_bytes=VMEM_LIMIT),
        name="legendre",
    )(starts, weights, logs, sines, coeffs, loads)


def block_of(device, group, devices):
    turned = jnp.where(group % 2 == 0, device, devices - 1 - device)
    return group * devices + turned


def order_layout(devices):
    groups = -(-(LMAX // GROUP) // devices)
    device, group, part, within = np.meshgrid(
        np.arange(devices), np.arange(groups), np.arange(2), np.arange(GROUP), indexing="ij"
    )
    block = group * devices + np.where(group % 2 == 0, device, devices - 1 - device)
    return groups, (block * GROUP + within).reshape(-1), part.reshape(-1)


def sector_table(orders, parts, cols):
    phases = (orders[:, None] * np.arange(cols)[None, :] % NLON) * (2.0 * np.pi / NLON)
    table = np.where(parts[:, None] == 0, np.cos(phases), -np.sin(phases))
    return np.where(orders[:, None] < LMAX, table, 0.0).astype(jnp.bfloat16)


def ring_table(table, tiles):
    ring = np.pad(table, ((0, 0), (0, tiles * 128 - table.shape[1])))
    return ring.reshape(-1, 128, tiles).transpose(0, 2, 1).reshape(ring.shape)


def start_logs():
    t = np.arange(LMAX, dtype=np.float64)
    terms = np.where(t > 0, 0.5 * np.log((2 * t + 1) / np.maximum(2 * t, 1)), 0.0)
    return np.cumsum(terms)


def recurrence(orders):
    degree = jnp.arange(HELD * CHUNK, dtype=jnp.float32).reshape(1, HELD, 1, CHUNK)
    order = orders.astype(jnp.float32)[:, None, :, None]
    gap = degree * degree - order * order
    one, two = degree >= order + 1.0, degree >= order + 2.0
    lead = jnp.where(one, (4.0 * degree * degree - 1.0) / jnp.where(one, gap, 1.0), 0.0)
    lag_num = (2.0 * degree + 1.0) * ((degree - 1.0) * (degree - 1.0) - order * order)
    lag = jnp.where(two, lag_num / jnp.where(two, (2.0 * degree - 3.0) * gap, 1.0), 0.0)
    lead = jnp.sqrt(lead)
    lag = jnp.where(one, jnp.sqrt(lag), -1.0)
    both = jnp.concatenate([lead, lag], axis=3)
    return jnp.pad(both, ((0, 0), (0, 0), (0, 0), (0, 128 - 2 * CHUNK)))


def cycle_geometry(row_ids, cycle_count):
    latitude = (row_ids.astype(jnp.float32) + 0.5) * (math.pi / cycle_count) - 0.5 * math.pi
    return (jnp.sin(latitude), jnp.cos(latitude))


def ring(axis, periodic):
    count = lax.axis_size(axis)
    forward = [(i, i + 1) for i in range(count - 1)]
    if periodic:
        forward.append((count - 1, 0))
    return forward, [(b, a) for a, b in forward]


def local(
    height,
    east_vel,
    north_vel,
    sea_depth,
    sea_mask,
    forcing,
    thickness,
    cycle_length,
    slot_order,
    love_index,
    love_table,
):
    rows, cols = height.shape
    lat_parts, lon_parts = lax.axis_size("lat"), lax.axis_size("lon")
    devices = lat_parts * lon_parts
    cycles = rows * lat_parts
    lat, lon = lax.axis_index("lat"), lax.axis_index("lon")
    bf16, f32 = jnp.bfloat16, jnp.float32

    row_ids = lat * rows + jnp.arange(rows, dtype=jnp.int32)
    inside = (row_ids > 0) & (row_ids < cycles - 1)

    tiles = tile_count(cols)
    natural = [x.T for x in (height, east_vel, north_vel, sea_depth, sea_mask)]
    forcing = forcing.transpose(0, 1, 3, 2)
    inside = jnp.where(inside, 1.0, 0.0)[None, :].astype(f32)
    eastward, westward = ring("lon", True)
    northward, southward = ring("lat", False)
    first, last = edges(thickness, natural, forcing, inside)
    west = lax.ppermute(last, "lon", eastward)
    east = lax.ppermute(first, "lon", westward)
    pushes = push(thickness, forcing)
    bands = range(rows // 128)
    arranged = [arrange(natural, pushes, east, west, inside, tiles, at) for at in bands]
    high = lax.ppermute(arranged[0][1], "lat", southward)
    low = lax.ppermute(arranged[-1][2], "lat", northward)
    fields = [band[0] for band in arranged]
    wide_rows = lat * rows - TOP + jnp.arange(TOP + rows + 32, dtype=jnp.int32)
    wide_sines, _ = cycle_geometry(wide_rows, cycles)
    spin = (time_step * coriolis_scale) * wide_sines
    spin = jnp.broadcast_to(spin[:, None], (TOP + rows + 32, 128))
    height, east, north, load = ocean(cols, fields, spin, low, high)

    groups, orders, parts = order_layout(devices)
    table = sector_table(orders, parts, cols)
    owned = devices * groups
    orders3 = jnp.asarray(orders.reshape(owned, 2, GROUP)[:, 0], jnp.int32)
    turn = (orders3 * (lon * cols) % NLON).astype(f32) * (2.0 * math.pi / NLON)
    turn_cos, turn_sin = jnp.cos(turn)[:, :, None], jnp.sin(turn)[:, :, None]
    spectra = lax.dot_general(
        jnp.asarray(ring_table(table, tiles)), load, (((1,), (1,)), ((), ())), preferred_element_type=f32
    ).reshape(owned, 2, GROUP, rows)
    spectra = jnp.stack(
        [
            turn_cos * spectra[:, 0] + turn_sin * spectra[:, 1],
            turn_cos * spectra[:, 1] - turn_sin * spectra[:, 0],
        ],
        axis=1,
    )
    _, cosines = cycle_geometry(row_ids, cycles)
    weight_lat = (0.5 / NLON) * cosines * (math.pi / cycles)
    retained = orders3[:, None, :, None] < cycle_length[None, None, None, :]
    weighted = jnp.where(retained, spectra * weight_lat, 0.0).astype(bf16)
    weighted = weighted.reshape(owned * 2 * GROUP, rows)
    mine = lax.all_to_all(weighted, ("lon", "lat"), 0, 0, tiled=True)
    mine = mine.reshape(lon_parts, lat_parts, groups * 2 * GROUP, rows).astype(f32).sum(axis=0)

    flip = jnp.asarray(np.eye(rows)[::-1].astype(bf16))
    hp = lat_parts // 2
    south = mine[:hp]
    north_side = jnp.dot(mine[hp:][::-1].astype(bf16), flip, preferred_element_type=f32)
    folded = jnp.stack([south + north_side, south - north_side])
    folded = folded.reshape(2, hp, groups, 2 * GROUP, rows).transpose(2, 0, 3, 1, 4)
    folded = folded.reshape(groups, 4 * GROUP, hp * rows)

    device = lon * lat_parts + lat
    starts = jnp.stack([block_of(device, g, devices) for g in range(groups)]).astype(jnp.int32)
    own_orders = starts[:, None] * GROUP + jnp.arange(GROUP, dtype=jnp.int32)[None, :]
    first_logs = jnp.asarray(
        np.pad(start_logs(), (0, owned * GROUP - LMAX)).astype(np.float32)
    )
    own_logs = jnp.stack(
        [lax.dynamic_slice(first_logs, (starts[g] * GROUP,), (GROUP,)) for g in range(groups)]
    )
    half_sines, half_cosines = cycle_geometry(jnp.arange(hp * rows, dtype=jnp.int32), cycles)
    z_start = own_logs[:, :, None] + own_orders.astype(f32)[:, :, None] * jnp.log(half_cosines)
    load_factor = jnp.sum(
        jnp.where(
            love_index[:, None] == jnp.arange(LOVE_ROWS, dtype=jnp.int32)[None, :],
            love_table[None, :],
            0.0,
        ),
        axis=1,
    )
    degree_load = jnp.pad(load_factor, (0, HELD * CHUNK - LMAX)).reshape(HELD, 1, CHUNK, 1)
    degree_load = jnp.broadcast_to(degree_load, (HELD, 1, CHUNK, GROUP)).reshape(HELD, 1, CROWS)
    synth, coeffs = legendre(
        starts,
        folded,
        z_start,
        jnp.broadcast_to(half_sines[None, :], (GROUP, hp * rows)),
        recurrence(own_orders),
        degree_load,
    )

    synth = synth.reshape(groups, 2, 2 * GROUP, hp, rows).transpose(1, 3, 0, 2, 4)
    synth = synth.reshape(2, hp, groups * 2 * GROUP, rows)
    south = (synth[0] + synth[1]).astype(bf16)
    north_side = jnp.dot(
        (synth[0] - synth[1]).astype(bf16), flip, preferred_element_type=f32
    ).astype(bf16)[::-1]
    share = LMAX // lat_parts
    coeffs = coeffs.reshape(groups, HELD, 2, CHUNK, GROUP).transpose(0, 2, 4, 1, 3)
    coeffs = coeffs.reshape(groups * 2 * GROUP, HELD * CHUNK)[:, :LMAX]
    coeffs = coeffs.reshape(groups * 2 * GROUP, lat_parts, share).transpose(1, 0, 2).astype(bf16)
    synth = jnp.concatenate([south, north_side]).reshape(lat_parts * groups * 2 * GROUP, rows)
    synth = lax.all_to_all(synth, "lat", 0, 0, tiled=True)
    def sectors(piece):
        held = [(lon, piece)]
        for shift in range(1, lon_parts):
            pairs = [(i, (i + shift) % lon_parts) for i in range(lon_parts)]
            held.append(((lon - shift) % lon_parts, lax.ppermute(piece, "lon", pairs)))
        return held

    per_sector = lat_parts * groups
    sector_waves = jnp.asarray(table.reshape(lon_parts, per_sector * 2 * GROUP, cols))
    sal_field = jnp.zeros((cols, rows), f32)
    gain = jnp.where(orders3 == 0, 1.0, 2.0)[:, :, None]
    cos_gain, sin_gain = gain * turn_cos, gain * turn_sin
    pieces = sectors(synth)
    for source, piece in pieces:
        own = lambda x: lax.dynamic_slice_in_dim(x, source * per_sector, per_sector, 0)
        cos_own, sin_own = own(cos_gain), own(sin_gain)
        piece = piece.reshape(per_sector, 2, GROUP, rows).astype(f32)
        piece = jnp.stack(
            [
                cos_own * piece[:, 0] - sin_own * piece[:, 1],
                sin_own * piece[:, 0] + cos_own * piece[:, 1],
            ],
            axis=1,
        ).astype(bf16).reshape(per_sector * 2 * GROUP, rows)
        waves = lax.dynamic_index_in_dim(sector_waves, source, 0, keepdims=False)
        sal_field = sal_field + lax.dot_general(
            waves, piece, (((0,), (0,)), ((), ())), preferred_element_type=f32
        )

    coeffs = coeffs.reshape(lat_parts * groups * 2 * GROUP, share)
    coeffs, _ = lax.optimization_barrier((coeffs, synth))
    coeffs = lax.all_to_all(coeffs, "lat", 0, 0, tiled=True)
    coeffs, _ = lax.optimization_barrier((coeffs, [piece for _, piece in pieces]))
    per_owner = LMAX // lon_parts
    own_slots = lax.dynamic_slice(slot_order, (lon * per_owner,), (per_owner,))
    load_coeffs = jnp.zeros((2, per_owner, share), f32)
    for source, piece in sectors(coeffs):
        own_orders = lax.dynamic_slice_in_dim(orders3, source * per_sector, per_sector, 0)
        found = own_slots[:, None] == own_orders.reshape(-1)[None, :]
        piece = piece.reshape(per_sector, 2, GROUP, share).transpose(1, 0, 2, 3)
        load_coeffs = load_coeffs + jnp.einsum(
            "qm,pmk->pqk",
            found.astype(bf16),
            piece.reshape(2, per_sector * GROUP, share),
            preferred_element_type=f32,
        )
    load_coeffs = math.sqrt(NLON * cycles) * load_coeffs
    return (height.T, east.T, north.T, load_coeffs, sal_field.T)


def solution(mesh):
    in_specs = (
        P("lat", "lon"),
        P("lat", "lon"),
        P("lat", "lon"),
        P("lat", "lon"),
        P("lat", "lon"),
        P(None, None, "lat", "lon"),
        P(),
        P("lat"),
        P(),
        P(),
        P(),
    )
    out_specs = (
        P("lat", "lon"),
        P("lat", "lon"),
        P("lat", "lon"),
        P(None, "lon", "lat"),
        P("lat", "lon"),
    )
    return jax.shard_map(local, mesh=mesh, in_specs=in_specs, out_specs=out_specs, check_vma=False)
```

```python
import functools
import math

import jax
import jax.numpy as jnp
import numpy as np
from jax import lax
from jax.experimental import pallas as pl
from jax.experimental.pallas import tpu as pltpu
from jax.sharding import PartitionSpec as P

NLON = 8640
LMAX = 720
LEVELS = 8
ITERS = 10
LOVE_ROWS = 64

time_step = 0.6
drag_coeff = 0.5
tide_speed = 0.1
coriolis_scale = 0.8

MARGIN = 2 * ITERS
STRIP = 24
TOP = 32
BT = 3
FIELDS = 7
WIDE = 4
GROUP = 8
CHUNK = 32
NCHUNK = -(-LMAX // CHUNK)
HELD = NCHUNK + 1
CROWS = CHUNK * GROUP
LIMIT = 1e10
SHRINK = 1e-20
SHRINK_LOG = 20.0 * math.log(10.0)
VMEM_LIMIT = 60 * 1024 * 1024


def tile_count(cols):
    tiles = -(-(cols + 2 * STRIP) // 128)
    while cols % tiles or cols // tiles % 8:
        tiles += 1
    return tiles


def wet_of(in_ref, mask):
    return jnp.where((in_ref[...] > 0.0) & (mask > 0), 1.0, 0.0)


def push_of(thick_ref, f_ref, part, where=slice(None)):
    total = thick_ref[0]
    pushed = total * f_ref[part, 0, where, :].astype(jnp.float32)
    for level in range(1, LEVELS):
        total = total + thick_ref[level]
        pushed += thick_ref[level] * f_ref[part, level, where, :].astype(jnp.float32)
    return pushed * (time_step / jnp.full((1, pushed.shape[1]), total, jnp.float32))


def edge_kernel(thick_ref, h_ref, e_ref, n_ref, d_ref, m_ref, f_ref, in_ref, out_ref):
    fields = (
        0.3 * h_ref[...], e_ref[...], n_ref[...], d_ref[...], wet_of(in_ref, m_ref[...]),
        push_of(thick_ref, f_ref, 0), push_of(thick_ref, f_ref, 1),
    )
    for v, field in enumerate(fields):
        out_ref[0, v] = field.astype(jnp.bfloat16)


def edges(weights, fields, forcing, inside):
    cols, rows = fields[0].shape
    at = lambda g: g * (cols // STRIP - 1)
    return pl.pallas_call(
        edge_kernel,
        grid=(2,),
        in_specs=[pl.BlockSpec(memory_space=pltpu.SMEM)]
        + [pl.BlockSpec((STRIP, rows), lambda g: (at(g), 0))] * 5
        + [pl.BlockSpec((2, LEVELS, STRIP, rows), lambda g: (0, 0, at(g), 0))]
        + [pl.BlockSpec(inside.shape, lambda g: (0, 0))],
        out_specs=pl.BlockSpec((1, FIELDS, STRIP, rows), lambda g: (g, 0, 0, 0)),
        out_shape=jax.ShapeDtypeStruct((2, FIELDS, STRIP, rows), jnp.bfloat16),
        name="edges",
    )(weights, *fields, forcing, inside)


def push_kernel(thick_ref, f_ref, out_ref):
    def part(i, carry):
        where = pl.ds(pl.multiple_of(i * STRIP, 8), STRIP)
        out_ref[0, where, :] = push_of(thick_ref, f_ref, 0, where)
        out_ref[1, where, :] = push_of(thick_ref, f_ref, 1, where)
        return carry

    lax.fori_loop(0, out_ref.shape[1] // STRIP, part, 0)


def push(weights, forcing):
    _, _, cols, rows = forcing.shape
    width = 15 * STRIP
    return pl.pallas_call(
        push_kernel,
        grid=(-(-cols // width),),
        in_specs=[
            pl.BlockSpec(memory_space=pltpu.SMEM),
            pl.BlockSpec((2, LEVELS, width, rows), lambda g: (0, 0, g, 0)),
        ],
        out_specs=pl.BlockSpec((2, width, rows), lambda g: (0, g, 0)),
        out_shape=jax.ShapeDtypeStruct((2, cols, rows), jnp.float32),
        compiler_params=pltpu.CompilerParams(vmem_limit_bytes=VMEM_LIMIT),
        cost_estimate=pl.CostEstimate(
            flops=32 * cols * rows, bytes_accessed=40 * cols * rows, transcendentals=0
        ),
        name="push",
    )(weights, forcing)


def arrange_kernel(
    tiles, h_ref, e_ref, n_ref, d_ref, m_ref, p_ref, east_ref, west_ref, in_ref,
    wide_ref, short_ref, first_ref, last_ref, halo_ref,
):
    lanes = h_ref.shape[0] // tiles

    @pl.when(pl.program_id(0) == 0)
    def start():
        halo_ref[...] = jnp.zeros(halo_ref.shape, jnp.float32)
        for v in range(FIELDS):
            halo_ref[v, :STRIP, :] = east_ref[v].astype(jnp.float32)
            halo_ref[v, halo_ref.shape[1] - STRIP :, :] = west_ref[v].astype(jnp.float32)

    for b in range(wide_ref.shape[1]):
        t = pl.program_id(0) * wide_ref.shape[1] + b
        rows = pl.ds(t, lanes, tiles)
        fields = (
            0.3 * h_ref[rows, :], e_ref[rows, :], n_ref[rows, :], d_ref[rows, :],
            wet_of(in_ref, m_ref[rows, :]), p_ref[0, rows, :], p_ref[1, rows, :],
        )
        for v, field in enumerate(fields):
            rest = halo_ref[v, pl.ds(t, 128 - lanes, tiles), :]
            turned = jnp.concatenate([field, rest], axis=0).T
            if v < WIDE:
                wide_ref[v, b] = turned
            else:
                short_ref[v - WIDE, b] = turned.astype(jnp.bfloat16)
            first_ref[v, b] = turned[:STRIP].astype(jnp.bfloat16)
            last_ref[v, b] = turned[128 - STRIP :].astype(jnp.bfloat16)


def arrange(fields, pushes, east, west, inside, tiles, at):
    cols, rows = fields[0].shape
    block = BT if tiles % BT == 0 else 1
    shape = lambda v, n, dtype: jax.ShapeDtypeStruct((v, tiles, n, 128), dtype)
    outs = [shape(WIDE, 128, jnp.float32), shape(FIELDS - WIDE, 128, jnp.bfloat16)]
    outs += [shape(FIELDS, STRIP, jnp.bfloat16)] * 2
    out_block = lambda x: pl.BlockSpec((x.shape[0], block) + x.shape[2:], lambda g: (0, g, 0, 0))
    halo_block = pl.BlockSpec((FIELDS, STRIP, 128), lambda g: (0, 0, at))
    return pl.pallas_call(
        functools.partial(arrange_kernel, tiles),
        grid=(tiles // block,),
        in_specs=[pl.BlockSpec((cols, 128), lambda g: (0, at))] * 5
        + [pl.BlockSpec((2, cols, 128), lambda g: (0, 0, at))]
        + [halo_block] * 2
        + [pl.BlockSpec((1, 128), lambda g: (0, at))],
        out_specs=[out_block(x) for x in outs],
        out_shape=outs,
        scratch_shapes=[pltpu.VMEM((FIELDS, tiles * 128 - cols, 128), jnp.float32)],
        compiler_params=pltpu.CompilerParams(vmem_limit_bytes=VMEM_LIMIT),
        cost_estimate=pl.CostEstimate(
            flops=64 * cols * 128, bytes_accessed=64 * cols * 128, transcendentals=0
        ),
        name="arrange",
    )(*fields, pushes, east, west, inside)


def ocean_kernel(nt, parts, *refs):
    field_refs, refs = refs[: 2 * parts], refs[2 * parts :]
    spin_ref, *refs = refs
    low_ref, high_ref, *refs = refs
    ho_ref, eo_ref, no_ref, lo_ref, *refs = refs
    H, E, N, PE, PN, K, D, A, FE, FN = refs
    step = pl.program_id(0)
    block = field_refs[0].shape[1]
    rows = parts * 128
    lanes = ho_ref.shape[0] // nt

    def put(t, where, height, east, north, depth, wet, push_e, push_n):
        is_wet = wet > 0.0
        H[t + 1, where, :] = height
        E[t, where, :] = east
        N[t, where, :] = north
        PE[t, where, :] = push_e
        PN[t, where, :] = push_n
        K[t, where, :] = jnp.where(is_wet, 0.3 / jnp.where(is_wet, depth, 1.0), jnp.inf)
        D[t, where, :] = depth
        A[t, where, :] = jnp.where(is_wet, 0.09, 0.0)
        FE[t + 1, where, :] = depth * east
        FN[t, where, :] = depth * north

    @pl.when(step < nt // block)
    def ingest():
        for b in range(block):
            t = step * block + b
            both = lambda refs: [
                ref[v, b].astype(jnp.float32) for ref in refs for v in range(ref.shape[0])
            ]
            for part in range(parts):
                where = slice(TOP + part * 128, TOP + (part + 1) * 128)
                put(t, where, *both(field_refs[2 * part : 2 * part + 2]))
            put(t, slice(TOP - STRIP, TOP), *both([low_ref]))
            put(t, slice(TOP + rows, TOP + rows + STRIP), *both([high_ref]))

    @pl.when(step == nt // block - 1)
    def run():
        def close(ref, tiles):
            for r in tiles:
                here = slice(r * 8, r * 8 + 8)
                ref[0, here, :] = pltpu.roll(ref[nt, here, :], 1, 1)
                ref[nt + 1, here, :] = pltpu.roll(ref[1, here, :], 127, 1)

        def substeps(first_tile, last_tile, count):
            tiles = range(first_tile, last_tile)

            def raise_height(t, carry):
                for r in tiles:
                    here = slice(r * 8, r * 8 + 8)
                    slope = FE[t + 2, here, :] - FE[t, here, :]
                    slope = slope + (FN[t, r * 8 + 1 : r * 8 + 9, :] - FN[t, r * 8 - 1 : r * 8 + 7, :])
                    H[t + 1, here, :] = H[t + 1, here, :] - A[t, here, :] * slope
                return carry

            def turn(t, carry):
                for r in tiles:
                    here = slice(r * 8, r * 8 + 8)
                    spin = spin_ref[here, :]
                    slope = H[t + 2, here, :] - H[t, here, :]
                    rise = H[t + 1, r * 8 + 1 : r * 8 + 9, :] - H[t + 1, r * 8 - 1 : r * 8 + 7, :]
                    east, north = E[t, here, :], N[t, here, :]
                    square = east * east + north * north + tide_speed * tide_speed
                    speed = square * lax.rsqrt(square)
                    damp = pl.reciprocal(1.0 + K[t, here, :] * speed, approx=True)
                    east_new = (east + spin * north - slope + PE[t, here, :]) * damp
                    north_new = (north - spin * east - rise + PN[t, here, :]) * damp
                    E[t, here, :] = east_new
                    N[t, here, :] = north_new
                    depth = D[t, here, :]
                    FE[t + 1, here, :] = depth * east_new
                    FN[t, here, :] = depth * north_new
                return carry

            def one(substep, carry):
                close(FE, tiles)
                lax.fori_loop(0, nt, raise_height, 0, unroll=BT)
                close(H, tiles)
                lax.fori_loop(0, nt, turn, 0, unroll=BT)
                return carry

            lax.fori_loop(0, count, one, 0)

        substep = 0
        while substep < ITERS:
            reach = lambda k: -(-(MARGIN - 2 * k - 1) // 8)
            count = 1
            while substep + count < ITERS and reach(substep + count) == reach(substep):
                count += 1
            substeps(TOP // 8 - reach(substep), (TOP + rows) // 8 + reach(substep), count)
            substep += count

    @pl.when(step >= nt // block - 1)
    def emit():
        first_row = pl.multiple_of(TOP + (step - (nt // block - 1)) * 128, 8)
        here = pl.ds(first_row, 128)
        for t in range(nt):
            where = pl.ds(t, lanes, nt)
            height = H[t + 1, here, :] * (1.0 / 0.3)
            ho_ref[where, :] = height.T[:lanes]
            eo_ref[where, :] = E[t, here, :].T[:lanes]
            no_ref[where, :] = N[t, here, :].T[:lanes]
            lo_ref[:, t * 128 : (t + 1) * 128] = jnp.where(A[t, here, :] > 0.0, height, 0.0).astype(
                jnp.bfloat16
            )


def ocean(cols, fields, spin, low, high):
    nt, rows = fields[0].shape[1], 64 * len(fields)
    block = BT if nt % BT == 0 else 1
    whole = lambda shape: pl.BlockSpec(
        shape, lambda g: (0,) * len(shape), pipeline_mode=pl.Buffered(1)
    )
    steps = nt // block
    by_tile = lambda x: pl.BlockSpec(
        (x.shape[0], block) + x.shape[2:], lambda g: (0, jnp.minimum(g, steps - 1), 0, 0)
    )
    band = lambda g: jnp.clip(g - (steps - 1), 0, rows // 128 - 1)
    out_block = pl.BlockSpec((cols, 128), lambda g: (0, band(g)))
    load_block = pl.BlockSpec((128, nt * 128), lambda g: (band(g), 0))
    outs = [jax.ShapeDtypeStruct((cols, rows), jnp.float32)] * 3
    outs.append(jax.ShapeDtypeStruct((rows, nt * 128), jnp.bfloat16))
    plain = pltpu.VMEM((nt, TOP + rows + 32, 128), jnp.float32)
    ringed = pltpu.VMEM((nt + 2, TOP + rows + 32, 128), jnp.float32)
    return pl.pallas_call(
        functools.partial(ocean_kernel, nt, len(fields) // 2),
        grid=(steps + rows // 128 - 1,),
        in_specs=[by_tile(x) for x in fields]
        + [whole(spin.shape)]
        + [by_tile(low), by_tile(high)],
        out_specs=[out_block] * 3 + [load_block],
        out_shape=outs,
        scratch_shapes=[ringed] + [plain] * 7 + [ringed, plain],
        compiler_params=pltpu.CompilerParams(vmem_limit_bytes=VMEM_LIMIT),
        name="ocean",
    )(*fields, spin, low, high)


def legendre_kernel(
    start_ref, w_ref, z_ref, s_ref, co_ref, l_ref, y_ref, c_ref,
    table_a, table_b, partial_a, partial_b, one, two, zed, scales, folded, spread,
):
    first_block = start_ref[pl.program_id(0)]
    lats = w_ref.shape[2]
    half = lats // 128
    y_ref[...] = jnp.zeros(y_ref.shape, jnp.float32)
    c_ref[...] = jnp.zeros(c_ref.shape, jnp.float32)
    table_b[...] = jnp.zeros(table_b.shape, jnp.bfloat16)
    partial_b[...] = jnp.zeros(partial_b.shape, jnp.float32)
    one[...] = jnp.ones(one.shape, jnp.float32)
    two[...] = jnp.ones(two.shape, jnp.float32)
    zed[...] = z_ref[0]
    row_ids = lax.broadcasted_iota(jnp.int32, (4 * GROUP, CROWS), 0)
    lane_ids = lax.broadcasted_iota(jnp.int32, (4 * GROUP, CROWS), 1)
    order_of = lane_ids % GROUP
    match = (row_ids % GROUP == order_of) & (
        row_ids // (2 * GROUP) == (lane_ids // GROUP + order_of) % 2
    )
    chosen = jnp.where(match, 1.0, 0.0)
    first_part = (row_ids // GROUP) % 2 == 0
    degree_of = (lane_ids // GROUP - order_of - first_block * GROUP)[:1]
    is_even = lax.broadcasted_iota(jnp.int32, (GROUP, lats), 0) % 2 == 0
    for p in range(2):
        even = w_ref[0, p * GROUP : (p + 1) * GROUP, :]
        odd = w_ref[0, (2 + p) * GROUP : (3 + p) * GROUP, :]
        folded[0, p] = jnp.where(is_even, even, odd)
        folded[1, p] = jnp.where(is_even, odd, even)

    def build(c, table, partial, between):
        pairs = co_ref[0, c]
        for q in range(2 * CHUNK):
            spread[q] = jnp.broadcast_to(pairs[:, q : q + 1], (GROUP, 128))
        tiles = [slice(t * 128, (t + 1) * 128) for t in range(half)]
        for part in range(CHUNK // 16):
            between(part)
            now, old = [one[:, x] for x in tiles], [two[:, x] for x in tiles]
            for t, lanes in enumerate(tiles):
                large = jnp.maximum(jnp.abs(now[t]), jnp.abs(old[t])) > LIMIT
                factor = jnp.where(large, SHRINK, 1.0)
                now[t], old[t] = now[t] * factor, old[t] * factor
                scale_log = zed[:, lanes] + jnp.where(large, SHRINK_LOG, 0.0)
                zed[:, lanes] = scale_log
                scales[:, lanes] = jnp.exp(scale_log)
            before = None
            for q in range(part * 16, part * 16 + 16):
                lead, lag = spread[q], spread[CHUNK + q]
                totals, rows = [None, None], []
                for t, lanes in enumerate(tiles):
                    value = (lead * s_ref[:, lanes]) * now[t] - lag * old[t]
                    old[t], now[t] = now[t], value
                    value = value * scales[:, lanes]
                    rows.append(value)
                    for p in range(2):
                        term = value * folded[q % 2, p, :, lanes]
                        totals[p] = term if t == 0 else totals[p] + term
                for p in range(2):
                    partial[p, q * GROUP : (q + 1) * GROUP, :] = totals[p]
                if q % 2:
                    for t, lanes in enumerate(tiles):
                        table[(q - 1) * GROUP : (q + 1) * GROUP, lanes] = jnp.concatenate(
                            [before[t], rows[t]], axis=0
                        ).astype(jnp.bfloat16)
                before = rows
            for t, lanes in enumerate(tiles):
                one[:, lanes], two[:, lanes] = now[t], old[t]

    def sums_of(c, partial):
        ones = jnp.ones((GROUP, 128), jnp.bfloat16)
        across = lambda x: lax.dot_general(
            ones, x, (((1,), (1,)), ((), ())), preferred_element_type=jnp.float32
        )
        gain = jnp.where(degree_of + c * CHUNK >= 0, l_ref[c], 0.0)
        sums = []
        for p in range(2):
            high = partial[p].astype(jnp.bfloat16)
            low = (partial[p] - high.astype(jnp.float32)).astype(jnp.bfloat16)
            total = (across(high) + across(low))[:1]
            total = jnp.where(gain != 0.0, total * gain, 0.0)
            c_ref[0, c, p : p + 1, :] = total
            sums.append(total)
        return (jnp.where(first_part, sums[0], sums[1]) * chosen).astype(jnp.bfloat16)

    def user(c, table, partial):
        held = []
        count = CHUNK // 16 - 1

        def piece(part):
            if part == 0:
                held.append(sums_of(c, partial))
            else:
                width = lats // count
                lanes = slice((part - 1) * width, part * width)
                y_ref[0, :, lanes] += jnp.dot(
                    held[0], table[:, lanes], preferred_element_type=jnp.float32
                )

        return piece

    first_chunk = first_block * GROUP // CHUNK

    def pair(i, carry):
        c = first_chunk + 2 * i
        build(c, table_a, partial_a, user(jnp.maximum(c - 1, 0), table_b, partial_b))
        build(c + 1, table_b, partial_b, user(c, table_a, partial_a))
        return carry

    count = jnp.maximum(NCHUNK - first_chunk + 1, 0) // 2
    lax.fori_loop(0, count, pair, 0)

    @pl.when(count > 0)
    def last():
        piece = user(first_chunk + 2 * count - 1, table_b, partial_b)
        for part in range(CHUNK // 16):
            piece(part)


def legendre(starts, weights, logs, sines, coeffs, loads):
    groups, _, lats = weights.shape
    by_group = lambda x: pl.BlockSpec(
        (1,) + x.shape[1:], lambda g: (g,) + (0,) * (x.ndim - 1)
    )
    whole = lambda x: pl.BlockSpec(x.shape, lambda g: (0,) * x.ndim)
    outs = [
        jax.ShapeDtypeStruct((groups, 4 * GROUP, lats), jnp.float32),
        jax.ShapeDtypeStruct((groups, HELD, 2, CROWS), jnp.float32),
    ]
    return pl.pallas_call(
        legendre_kernel,
        grid=(groups,),
        in_specs=[
            pl.BlockSpec(memory_space=pltpu.SMEM),
            by_group(weights),
            by_group(logs),
            whole(sines),
            by_group(coeffs),
            whole(loads),
        ],
        out_specs=[by_group(x) for x in outs],
        out_shape=outs,
        scratch_shapes=[
            pltpu.VMEM((CROWS, lats), jnp.bfloat16),
            pltpu.VMEM((CROWS, lats), jnp.bfloat16),
            pltpu.VMEM((2, CROWS, 128), jnp.float32),
            pltpu.VMEM((2, CROWS, 128), jnp.float32),
            pltpu.VMEM((GROUP, lats), jnp.float32),
            pltpu.VMEM((GROUP, lats), jnp.float32),
            pltpu.VMEM((GROUP, lats), jnp.float32),
            pltpu.VMEM((GROUP, lats), jnp.float32),
            pltpu.VMEM((2, 2, GROUP, lats), jnp.float32),
            pltpu.VMEM((2 * CHUNK, GROUP, 128), jnp.float32),
        ],
        compiler_params=pltpu.CompilerParams(vmem_limit_bytes=VMEM_LIMIT),
        name="legendre",
    )(starts, weights, logs, sines, coeffs, loads)


def block_of(device, group, devices):
    turned = jnp.where(group % 2 == 0, device, devices - 1 - device)
    return group * devices + turned


def order_layout(devices):
    groups = -(-(LMAX // GROUP) // devices)
    device, group, part, within = np.meshgrid(
        np.arange(devices), np.arange(groups), np.arange(2), np.arange(GROUP), indexing="ij"
    )
    block = group * devices + np.where(group % 2 == 0, device, devices - 1 - device)
    return groups, (block * GROUP + within).reshape(-1), part.reshape(-1)


def sector_table(orders, parts, cols):
    phases = (orders[:, None] * np.arange(cols)[None, :] % NLON) * (2.0 * np.pi / NLON)
    table = np.where(parts[:, None] == 0, np.cos(phases), -np.sin(phases))
    return np.where(orders[:, None] < LMAX, table, 0.0).astype(jnp.bfloat16)


def ring_table(table, tiles):
    ring = np.pad(table, ((0, 0), (0, tiles * 128 - table.shape[1])))
    return ring.reshape(-1, 128, tiles).transpose(0, 2, 1).reshape(ring.shape)


def start_logs():
    t = np.arange(LMAX, dtype=np.float64)
    terms = np.where(t > 0, 0.5 * np.log((2 * t + 1) / np.maximum(2 * t, 1)), 0.0)
    return np.cumsum(terms)


def recurrence(orders):
    degree = jnp.arange(HELD * CHUNK, dtype=jnp.float32).reshape(1, HELD, 1, CHUNK)
    order = orders.astype(jnp.float32)[:, None, :, None]
    gap = degree * degree - order * order
    one, two = degree >= order + 1.0, degree >= order + 2.0
    lead = jnp.where(one, (4.0 * degree * degree - 1.0) / jnp.where(one, gap, 1.0), 0.0)
    lag_num = (2.0 * degree + 1.0) * ((degree - 1.0) * (degree - 1.0) - order * order)
    lag = jnp.where(two, lag_num / jnp.where(two, (2.0 * degree - 3.0) * gap, 1.0), 0.0)
    lead = jnp.sqrt(lead)
    lag = jnp.where(one, jnp.sqrt(lag), -1.0)
    both = jnp.concatenate([lead, lag], axis=3)
    return jnp.pad(both, ((0, 0), (0, 0), (0, 0), (0, 128 - 2 * CHUNK)))


def cycle_geometry(row_ids, cycle_count):
    latitude = (row_ids.astype(jnp.float32) + 0.5) * (math.pi / cycle_count) - 0.5 * math.pi
    return (jnp.sin(latitude), jnp.cos(latitude))


def ring(axis, periodic):
    count = lax.axis_size(axis)
    forward = [(i, i + 1) for i in range(count - 1)]
    if periodic:
        forward.append((count - 1, 0))
    return forward, [(b, a) for a, b in forward]


def local(
    height,
    east_vel,
    north_vel,
    sea_depth,
    sea_mask,
    forcing,
    thickness,
    cycle_length,
    slot_order,
    love_index,
    love_table,
):
    rows, cols = height.shape
    lat_parts, lon_parts = lax.axis_size("lat"), lax.axis_size("lon")
    devices = lat_parts * lon_parts
    cycles = rows * lat_parts
    lat, lon = lax.axis_index("lat"), lax.axis_index("lon")
    bf16, f32 = jnp.bfloat16, jnp.float32

    row_ids = lat * rows + jnp.arange(rows, dtype=jnp.int32)
    inside = (row_ids > 0) & (row_ids < cycles - 1)

    tiles = tile_count(cols)
    natural = [x.T for x in (height, east_vel, north_vel, sea_depth, sea_mask)]
    forcing = forcing.transpose(0, 1, 3, 2)
    inside = jnp.where(inside, 1.0, 0.0)[None, :].astype(f32)
    eastward, westward = ring("lon", True)
    northward, southward = ring("lat", False)
    first, last = edges(thickness, natural, forcing, inside)
    west = lax.ppermute(last, "lon", eastward)
    east = lax.ppermute(first, "lon", westward)
    pushes = push(thickness, forcing)
    bands = range(rows // 128)
    arranged = [arrange(natural, pushes, east, west, inside, tiles, at) for at in bands]
    high = lax.ppermute(arranged[0][2], "lat", southward)
    low = lax.ppermute(arranged[-1][3], "lat", northward)
    fields = [x for band in arranged for x in band[:2]]
    wide_rows = lat * rows - TOP + jnp.arange(TOP + rows + 32, dtype=jnp.int32)
    wide_sines, _ = cycle_geometry(wide_rows, cycles)
    spin = (time_step * coriolis_scale) * wide_sines
    spin = jnp.broadcast_to(spin[:, None], (TOP + rows + 32, 128))
    height, east, north, load = ocean(cols, fields, spin, low, high)

    groups, orders, parts = order_layout(devices)
    table = sector_table(orders, parts, cols)
    owned = devices * groups
    orders3 = jnp.asarray(orders.reshape(owned, 2, GROUP)[:, 0], jnp.int32)
    turn = (orders3 * (lon * cols) % NLON).astype(f32) * (2.0 * math.pi / NLON)
    turn_cos, turn_sin = jnp.cos(turn)[:, :, None], jnp.sin(turn)[:, :, None]
    spectra = lax.dot_general(
        jnp.asarray(ring_table(table, tiles)), load, (((1,), (1,)), ((), ())), preferred_element_type=f32
    ).reshape(owned, 2, GROUP, rows)
    spectra = jnp.stack(
        [
            turn_cos * spectra[:, 0] + turn_sin * spectra[:, 1],
            turn_cos * spectra[:, 1] - turn_sin * spectra[:, 0],
        ],
        axis=1,
    )
    _, cosines = cycle_geometry(row_ids, cycles)
    weight_lat = (0.5 / NLON) * cosines * (math.pi / cycles)
    retained = orders3[:, None, :, None] < cycle_length[None, None, None, :]
    weighted = jnp.where(retained, spectra * weight_lat, 0.0).astype(bf16)
    weighted = weighted.reshape(owned * 2 * GROUP, rows)
    mine = lax.all_to_all(weighted, ("lon", "lat"), 0, 0, tiled=True)
    mine = mine.reshape(lon_parts, lat_parts, groups * 2 * GROUP, rows).astype(f32).sum(axis=0)

    flip = jnp.asarray(np.eye(rows)[::-1].astype(bf16))
    hp = lat_parts // 2
    south = mine[:hp]
    north_side = jnp.dot(mine[hp:][::-1].astype(bf16), flip, preferred_element_type=f32)
    folded = jnp.stack([south + north_side, south - north_side])
    folded = folded.reshape(2, hp, groups, 2 * GROUP, rows).transpose(2, 0, 3, 1, 4)
    folded = folded.reshape(groups, 4 * GROUP, hp * rows)

    device = lon * lat_parts + lat
    starts = jnp.stack([block_of(device, g, devices) for g in range(groups)]).astype(jnp.int32)
    own_orders = starts[:, None] * GROUP + jnp.arange(GROUP, dtype=jnp.int32)[None, :]
    first_logs = jnp.asarray(
        np.pad(start_logs(), (0, owned * GROUP - LMAX)).astype(np.float32)
    )
    own_logs = jnp.stack(
        [lax.dynamic_slice(first_logs, (starts[g] * GROUP,), (GROUP,)) for g in range(groups)]
    )
    half_sines, half_cosines = cycle_geometry(jnp.arange(hp * rows, dtype=jnp.int32), cycles)
    z_start = own_logs[:, :, None] + own_orders.astype(f32)[:, :, None] * jnp.log(half_cosines)
    load_factor = jnp.sum(
        jnp.where(
            love_index[:, None] == jnp.arange(LOVE_ROWS, dtype=jnp.int32)[None, :],
            love_table[None, :],
            0.0,
        ),
        axis=1,
    )
    degree_load = jnp.pad(load_factor, (0, HELD * CHUNK - LMAX)).reshape(HELD, 1, CHUNK, 1)
    degree_load = jnp.broadcast_to(degree_load, (HELD, 1, CHUNK, GROUP)).reshape(HELD, 1, CROWS)
    synth, coeffs = legendre(
        starts,
        folded,
        z_start,
        jnp.broadcast_to(half_sines[None, :], (GROUP, hp * rows)),
        recurrence(own_orders),
        degree_load,
    )

    synth = synth.reshape(groups, 2, 2 * GROUP, hp, rows).transpose(1, 3, 0, 2, 4)
    synth = synth.reshape(2, hp, groups * 2 * GROUP, rows)
    south = (synth[0] + synth[1]).astype(bf16)
    north_side = jnp.dot(
        (synth[0] - synth[1]).astype(bf16), flip, preferred_element_type=f32
    ).astype(bf16)[::-1]
    share = LMAX // lat_parts
    coeffs = coeffs.reshape(groups, HELD, 2, CHUNK, GROUP).transpose(0, 2, 4, 1, 3)
    coeffs = coeffs.reshape(groups * 2 * GROUP, HELD * CHUNK)[:, :LMAX]
    coeffs = coeffs.reshape(groups * 2 * GROUP, lat_parts, share).transpose(1, 0, 2).astype(bf16)
    synth = jnp.concatenate([south, north_side]).reshape(lat_parts * groups * 2 * GROUP, rows)
    synth = lax.all_to_all(synth, "lat", 0, 0, tiled=True)
    def sectors(piece):
        held = [(lon, piece)]
        for shift in range(1, lon_parts):
            pairs = [(i, (i + shift) % lon_parts) for i in range(lon_parts)]
            held.append(((lon - shift) % lon_parts, lax.ppermute(piece, "lon", pairs)))
        return held

    per_sector = lat_parts * groups
    sector_waves = jnp.asarray(table.reshape(lon_parts, per_sector * 2 * GROUP, cols))
    sal_field = jnp.zeros((cols, rows), f32)
    gain = jnp.where(orders3 == 0, 1.0, 2.0)[:, :, None]
    cos_gain, sin_gain = gain * turn_cos, gain * turn_sin
    pieces = sectors(synth)
    for source, piece in pieces:
        own = lambda x: lax.dynamic_slice_in_dim(x, source * per_sector, per_sector, 0)
        cos_own, sin_own = own(cos_gain), own(sin_gain)
        piece = piece.reshape(per_sector, 2, GROUP, rows).astype(f32)
        piece = jnp.stack(
            [
                cos_own * piece[:, 0] - sin_own * piece[:, 1],
                sin_own * piece[:, 0] + cos_own * piece[:, 1],
            ],
            axis=1,
        ).astype(bf16).reshape(per_sector * 2 * GROUP, rows)
        waves = lax.dynamic_index_in_dim(sector_waves, source, 0, keepdims=False)
        sal_field = sal_field + lax.dot_general(
            waves, piece, (((0,), (0,)), ((), ())), preferred_element_type=f32
        )

    coeffs = coeffs.reshape(lat_parts * groups * 2 * GROUP, share)
    coeffs, _ = lax.optimization_barrier((coeffs, synth))
    coeffs = lax.all_to_all(coeffs, "lat", 0, 0, tiled=True)
    coeffs, _ = lax.optimization_barrier((coeffs, [piece for _, piece in pieces]))
    per_owner = LMAX // lon_parts
    own_slots = lax.dynamic_slice(slot_order, (lon * per_owner,), (per_owner,))
    load_coeffs = jnp.zeros((2, per_owner, share), f32)
    for source, piece in sectors(coeffs):
        own_orders = lax.dynamic_slice_in_dim(orders3, source * per_sector, per_sector, 0)
        found = own_slots[:, None] == own_orders.reshape(-1)[None, :]
        piece = piece.reshape(per_sector, 2, GROUP, share).transpose(1, 0, 2, 3)
        load_coeffs = load_coeffs + jnp.einsum(
            "qm,pmk->pqk",
            found.astype(bf16),
            piece.reshape(2, per_sector * GROUP, share),
            preferred_element_type=f32,
        )
    load_coeffs = math.sqrt(NLON * cycles) * load_coeffs
    return (height.T, east.T, north.T, load_coeffs, sal_field.T)


def solution(mesh):
    in_specs = (
        P("lat", "lon"),
        P("lat", "lon"),
        P("lat", "lon"),
        P("lat", "lon"),
        P("lat", "lon"),
        P(None, None, "lat", "lon"),
        P(),
        P("lat"),
        P(),
        P(),
        P(),
    )
    out_specs = (
        P("lat", "lon"),
        P("lat", "lon"),
        P("lat", "lon"),
        P(None, "lon", "lat"),
        P("lat", "lon"),
    )
    return jax.shard_map(local, mesh=mesh, in_specs=in_specs, out_specs=out_specs, check_vma=False)
```
